256 devices in a mesh: row: 32 (over y, z_lo, core), col: 8 (over z_hi, x).
Axes of the slice: x: 4, y: 4, z: 8 (z_hi: 2, z_lo: 4; z = z_hi * 4 + z_lo), core: 2. Of those that a mesh axis runs over, the one named last changes fastest.
Arguments:
- tokens_in: bfloat16 [3584, 3072], P(None, 'row'), may hold values from -6 to 6
- out_grad: bfloat16 [3584, 3072], P('col', 'row'), may hold values from -0.100097656 to 0.100097656
- pre_act: bfloat16 [3584, 12288], P('row', 'col'), may hold values from -8 to 8
- w_down: bfloat16 [3072, 12288], P('row', 'col'), may hold values from -0.0546875 to 0.0546875
Outputs:
- grad_up: float32 [3072, 12288], P('row', 'col')
- grad_down: float32 [3072, 12288], P('row', 'col')
The draws below stay inside these ranges and needn't reach their ends.
All inputs are finite; a program needn't handle non-finite values.
Results may differ from the reference program's by a relative error of at most 0.0029.
Values may be sent and summed in bfloat16 or wider, within the bound.
No kernel may reach another device: no remote copies, remote signals or barrier semaphores. Data moves between devices by JAX's collectives and lax.ppermute only.
A program may use at most 128 MiB of HBM per device.

```python
import math
import jax
import jax.numpy as jnp

D = 3072
FF = 12288
TOKENS = 3584


def levels(stream_key, dims, split, least, top_value):
    def one(position, parts):
        heights = jax.random.uniform(jax.random.fold_in(jax.random.fold_in(stream_key, 6), position), (parts,), jnp.float32, least / len(split), top_value / len(split))
        return jnp.repeat(jnp.exp(heights), dims[position] // parts).reshape((-1,) + (1,) * (len(dims) - position - 1))

    gain = one(*split[0])
    for cut in split[1:]:
        gain = gain * one(*cut)
    return gain


def noise(rng, shape, spread, reach, pieces=(), kind=jnp.bfloat16):
    level = levels(rng, shape, pieces, -0.22, 0.18) if pieces else 1.0
    result = jax.random.normal(rng, shape, jnp.float32) * spread * level
    return jnp.minimum(jnp.maximum(result, -reach), reach).astype(kind)


def setup_inputs(seed: int = 0) -> dict:
    splits = jax.random.split(jax.random.key(seed), 5)
    tokens_in = noise(splits[0], (TOKENS, D), 1.0, 6.0, ((1, 32),))
    out_grad = noise(splits[1], (TOKENS, D), (TOKENS ** -0.5), 0.100097656, ((0, 8), (1, 32)))
    pre_act = noise(splits[2], (TOKENS, FF), 1.5, 8.0, ((0, 32), (1, 8)))
    w_down = noise(splits[3], (D, FF), FF ** -0.5, 0.0546875, ((0, 32), (1, 8)))
    return {"tokens_in": tokens_in, "out_grad": out_grad, "pre_act": pre_act, "w_down": w_down}


def gelu_parts(pre):
    scale_c = math.sqrt(2.0 / math.pi)
    inner = jnp.tanh(scale_c * (pre + 0.044715 * pre * pre * pre))
    active = 0.5 * pre * (1.0 + inner)
    slope = 0.5 * (1.0 + inner) + 0.5 * pre * (1.0 - inner * inner) * scale_c * (1.0 + 3.0 * 0.044715 * pre * pre)
    return (active, slope)

def reference(tokens_in, out_grad, pre_act, w_down):
    hid_grad = jnp.dot(out_grad, w_down, preferred_element_type=jnp.float32)
    active, slope = gelu_parts(pre_act.astype(jnp.float32))
    act_half = active.astype(jnp.bfloat16)
    pre_grad = (hid_grad * slope).astype(jnp.bfloat16)
    grad_up = jnp.dot(tokens_in.T, pre_grad, preferred_element_type=jnp.float32)
    grad_down = jnp.dot(out_grad.T, act_half, preferred_element_type=jnp.float32)
    return (grad_up, grad_down)
```

```python
import math

import jax
import jax.numpy as jnp
from jax import lax
from jax.sharding import Mesh
from jax.sharding import PartitionSpec as P

ROW = ("y", "zl", "core")
COL = ("zh", "x")
bf16, f32 = jnp.bfloat16, jnp.float32


def gelu_parts(pre):
    scale_c = math.sqrt(2.0 / math.pi)
    inner = jnp.tanh(scale_c * (pre + 0.044715 * pre * pre * pre))
    active = 0.5 * pre * (1.0 + inner)
    slope = 0.5 * (1.0 + inner) + 0.5 * pre * (1.0 - inner * inner) * scale_c * (
        1.0 + 3.0 * 0.044715 * pre * pre
    )
    return (active, slope)


def shift(v, axis, by, size=4):
    return lax.ppermute(v, axis, [(i, (i + by) % size) for i in range(size)])


def ring_gather(v, axis):
    half = v.shape[0] // 2
    before = shift(v, axis, 1)
    after = shift(v, axis, -1)
    far = jnp.concatenate([shift(before[:half], axis, 1), shift(after[half:], axis, -1)])
    return [v, after, far, before]


def pair(first, mine, other):
    return jnp.where(first, mine, other), jnp.where(first, other, mine)


def spread_sum(part, zl):
    n = part.shape[0] // 4
    total = part[:n]
    for r in (1, 3, 2):
        total = total + shift(part[r * n : (r + 1) * n].astype(bf16), "zl", r).astype(f32)
    return total


def body(tokens_in, out_grad, pre_act, w_down):
    y, zl, core, zh, x = (lax.axis_index(a) for a in ("y", "zl", "core", "zh", "x"))
    first = core == 0
    kd, full = w_down.shape
    kt = pre_act.shape[0]
    half = full // 2

    rows = jnp.concatenate([w_down, pre_act])
    low, high = rows[:, :half], rows[:, half:]
    mine, theirs = jnp.where(first, low, high), jnp.where(first, high, low)
    lo, hi = pair(first, mine, shift(theirs, "core", 1, 2))
    w_own = jnp.concatenate([lo[:kd], hi[:kd]])
    pre = jnp.concatenate([lo[kd:], hi[kd:]]).astype(f32)
    active, slope = gelu_parts(pre)

    q = (x + y) % 4
    perms = ([], [])
    for yy in range(4):
        for hh in range(2):
            for xx in range(4):
                qq = (xx + yy) % 4
                for k in range(2):
                    src = (yy * 2 + qq // 2) * 4 + 2 * (qq % 2) + (hh + k) % 2
                    perms[k].append((src, (yy * 2 + hh) * 4 + xx))
    r1, r2 = (lax.ppermute(out_grad, ("y", "zh", "x"), p) for p in perms)
    og_q = jnp.concatenate([jnp.where(zh == 0, r1, r2), jnp.where(zh == 0, r2, r1)])
    quarter = og_q.shape[0]
    tok_q = lax.dynamic_slice_in_dim(tokens_in, q * quarter, quarter, 0)
    both = jnp.stack([tok_q, og_q]).reshape(2, 4, 2, kt, kd)
    mine = jnp.where(first, both[:, :, 0], both[:, :, 1])
    theirs = jnp.where(first, both[:, :, 1], both[:, :, 0])
    lo, hi = pair(first, mine, shift(theirs, "core", 1, 2))
    both = jnp.concatenate([lo, hi], -1)
    got = [lax.dynamic_index_in_dim(both, (zl - r) % 4, 1, False) for r in range(4)]
    got = [got[0]] + [shift(got[r], "zl", -r) for r in range(1, 4)]
    both = jnp.concatenate(got, -1)
    moves = [(yy * 4 + xx, (yy + xx) % 4 * 4 + xx) for yy in range(4) for xx in range(4)]
    turned = lax.ppermute(both[1], ("y", "x"), moves)
    three = jnp.concatenate([both[0], both[1], turned])
    slots = ring_gather(three, "x")
    buf = jnp.zeros((4,) + three.shape, bf16)
    for r in range(4):
        buf = lax.dynamic_update_slice_in_dim(buf, slots[r][None], (x + r) % 4, 0)
    buf = buf.reshape(4, 3, kt, three.shape[1])
    lo, hi = pair(first, buf, shift(buf, "core", 1, 2))
    buf = jnp.concatenate([lo, hi], 2)
    tok = buf[:, 0].reshape(-1, three.shape[1])
    og = buf[:, 1].reshape(-1, three.shape[1])

    near = {r: shift(w_own, "zl", -r) for r in (1, 3, 2)}
    g0 = ring_gather(jnp.concatenate([w_own, active.astype(bf16)]), "y")
    g1 = ring_gather(jnp.concatenate([near[1], near[3]]), "y")
    g2 = ring_gather(near[2], "y")
    nd = w_own.shape[0]

    act_all = jnp.concatenate([g[nd:] for g in g0])
    down = spread_sum(lax.dot_general(og, act_all, (((0,), (0,)), ((), ())), preferred_element_type=f32), zl)

    hid = None
    for r in range(4):
        w_r = jnp.concatenate([g0[r][:nd], g1[r][:nd], g2[r], g1[r][nd:]])
        term = jnp.dot(buf[(4 - r) % 4, 2], w_r, preferred_element_type=f32)
        hid = term if hid is None else hid + term
    pre_grad = (hid * slope).astype(bf16)
    grad_all = jnp.concatenate(ring_gather(pre_grad, "y"))
    up = spread_sum(lax.dot_general(tok, grad_all, (((0,), (0,)), ((), ())), preferred_element_type=f32), zl)

    outs = []
    for total in (up, down):
        a, b = total[:kd], total[kd:]
        mine, theirs = jnp.where(first, a, b), jnp.where(first, b, a)
        outs.append(jnp.concatenate(pair(first, mine, shift(theirs, "core", 1, 2)), 1))
    return tuple(outs)


def solution(mesh):
    fine = Mesh(mesh.devices.reshape(4, 4, 2, 2, 4), ROW + COL)
    return jax.shard_map(
        body,
        mesh=fine,
        in_specs=(P(None, ROW), P(COL, ROW), P(ROW, COL), P(ROW, COL)),
        out_specs=(P(ROW, COL), P(ROW, COL)),
        check_vma=False,
    )
```

```python
import math

import jax
import jax.numpy as jnp
from jax import lax
from jax.sharding import Mesh
from jax.sharding import PartitionSpec as P

ROW = ("y", "zl", "core")
COL = ("zh", "x")
bf16, f32 = jnp.bfloat16, jnp.float32
tie = lax.optimization_barrier


def gelu_parts(pre):
    scale_c = math.sqrt(2.0 / math.pi)
    inner = jnp.tanh(scale_c * (pre + 0.044715 * pre * pre * pre))
    active = 0.5 * pre * (1.0 + inner)
    slope = 0.5 * (1.0 + inner) + 0.5 * pre * (1.0 - inner * inner) * scale_c * (
        1.0 + 3.0 * 0.044715 * pre * pre
    )
    return (active, slope)


def shift(v, axis, by, size=4):
    return lax.ppermute(v, axis, [(i, (i + by) % size) for i in range(size)])


def ring_first(v, axis):
    return shift(v, axis, 1), shift(v, axis, -1)


def ring_second(v, before, after, axis):
    half = v.shape[0] // 2
    far = jnp.concatenate([shift(before[:half], axis, 1), shift(after[half:], axis, -1)])
    return [v, after, far, before]


def pair(first, mine, other):
    return jnp.where(first, mine, other), jnp.where(first, other, mine)


def spread(part):
    n = part.shape[0] // 4
    with jax.named_scope("spread"):
        return part[:n], [shift(part[r * n : (r + 1) * n].astype(bf16), "zl", r) for r in (1, 3, 2)]


def dot_t(a, b):
    return lax.dot_general(a, b, (((0,), (0,)), ((), ())), preferred_element_type=f32)


def body(tokens_in, out_grad, pre_act, w_down):
    y, zl, core, zh, x = (lax.axis_index(a) for a in ("y", "zl", "core", "zh", "x"))
    first = core == 0
    kd, full = w_down.shape
    kt = pre_act.shape[0]
    half = full // 2

    with jax.named_scope("swap_w_pre"):
        rows = jnp.concatenate([w_down, pre_act])
        low, high = rows[:, :half], rows[:, half:]
        mine, theirs = jnp.where(first, low, high), jnp.where(first, high, low)
        lo, hi = pair(first, mine, shift(theirs, "core", 1, 2))
        w_own = jnp.concatenate([lo[:kd], hi[:kd]])
        pre = jnp.concatenate([lo[kd:], hi[kd:]])

    with jax.named_scope("quarter"):
        q = (x + y) % 4
        perms = ([], [])
        for yy in range(4):
            for hh in range(2):
                for xx in range(4):
                    qq = (xx + yy) % 4
                    for k in range(2):
                        src = (yy * 2 + qq // 2) * 4 + 2 * (qq % 2) + (hh + k) % 2
                        perms[k].append((src, (yy * 2 + hh) * 4 + xx))
        r1, r2 = (lax.ppermute(out_grad, ("y", "zh", "x"), p) for p in perms)
        w_own, pre, r1, r2 = tie((w_own, pre, r1, r2))
        active, slope = gelu_parts(pre.astype(f32))
        act = active.astype(bf16)
        og_q = jnp.concatenate([jnp.where(zh == 0, r1, r2), jnp.where(zh == 0, r2, r1)])
        quarter = og_q.shape[0]
        tok_q = lax.dynamic_slice_in_dim(tokens_in, q * quarter, quarter, 0)
    with jax.named_scope("w_zl"):
        near = {r: shift(w_own, "zl", -r) for r in (1, 3, 2)}
    with jax.named_scope("og_swap"):
        both = jnp.stack([tok_q, og_q]).reshape(2, 4, 2, kt, kd)
        mine = jnp.where(first, both[:, :, 0], both[:, :, 1])
        theirs = jnp.where(first, both[:, :, 1], both[:, :, 0])
        lo, hi = pair(first, mine, shift(theirs, "core", 1, 2))
    with jax.named_scope("og_zl"):
        both = jnp.concatenate([lo, hi], -1)
        got = [lax.dynamic_index_in_dim(both, (zl - r) % 4, 1, False) for r in range(4)]
        got = [got[0]] + [shift(got[r], "zl", -r) for r in range(1, 4)]
    with jax.named_scope("act_y"):
        v0 = jnp.concatenate([w_own, act])
        b0, a0 = ring_first(v0, "y")
    with jax.named_scope("fence1"):
        v0, b0, a0, near, got = tie((v0, b0, a0, near, got))
    with jax.named_scope("act_y2"):
        g0 = ring_second(v0, b0, a0, "y")
    with jax.named_scope("w_y"):
        v1 = jnp.concatenate([near[1], near[2], near[3]])
        b1, a1 = ring_first(v1, "y")
    with jax.named_scope("og_turn"):
        both = jnp.concatenate(got, -1)
        moves = [(yy * 4 + xx, (yy + xx) % 4 * 4 + xx) for yy in range(4) for xx in range(4)]
        turned = lax.ppermute(both[1], ("y", "x"), moves)
    with jax.named_scope("og_x"):
        three = jnp.concatenate([both[0], both[1], turned])
        b3, a3 = ring_first(three, "x")
        slots = ring_second(three, b3, a3, "x")
    with jax.named_scope("fence2"):
        slots, b1, a1, g0 = tie((slots, b1, a1, g0))
    with jax.named_scope("w_y2"):
        g1 = ring_second(v1, b1, a1, "y")
    with jax.named_scope("og_core"):
        buf = jnp.zeros((4,) + three.shape, bf16)
        for r in range(4):
            buf = lax.dynamic_update_slice_in_dim(buf, slots[r][None], (x + r) % 4, 0)
        buf = buf.reshape(4, 3, kt, three.shape[1])
        lo, hi = pair(first, buf, shift(buf, "core", 1, 2))
        buf = jnp.concatenate([lo, hi], 2)
        tok = buf[:, 0].reshape(-1, three.shape[1])
        og = buf[:, 1].reshape(-1, three.shape[1])
    nd = w_own.shape[0]

    with jax.named_scope("down"):
        act_all = jnp.concatenate([g[nd:] for g in g0])
        down, parts = spread(dot_t(og, act_all))
    with jax.named_scope("fence3"):
        g1, down, parts = tie((g1, down, parts))
        for p in parts:
            down = down + p.astype(f32)

    with jax.named_scope("hid"):
        hid = None
        for r in range(4):
            w_r = jnp.concatenate([g0[r][:nd], g1[r]])
            term = jnp.dot(buf[(4 - r) % 4, 2], w_r, preferred_element_type=f32)
            hid = term if hid is None else hid + term
        pre_grad = (hid * slope).astype(bf16)
    with jax.named_scope("grad_y"):
        bb, aa = ring_first(pre_grad, "y")
        grad_all = jnp.concatenate(ring_second(pre_grad, bb, aa, "y"))
    with jax.named_scope("up"):
        up, parts = spread(dot_t(tok, grad_all))
        for p in parts:
            up = up + p.astype(f32)

    outs = []
    with jax.named_scope("swap_out"):
        for total in (up, down):
            a, b = total[:kd], total[kd:]
            mine, theirs = jnp.where(first, a, b), jnp.where(first, b, a)
            outs.append(jnp.concatenate(pair(first, mine, shift(theirs, "core", 1, 2)), 1))
    return tuple(outs)


def solution(mesh):
    fine = Mesh(mesh.devices.reshape(4, 4, 2, 2, 4), ROW + COL)
    return jax.shard_map(
        body,
        mesh=fine,
        in_specs=(P(None, ROW), P(COL, ROW), P(ROW, COL), P(ROW, COL)),
        out_specs=(P(ROW, COL), P(ROW, COL)),
        check_vma=False,
    )
```

```python
import math

import jax
import jax.numpy as jnp
from jax import lax
from jax.sharding import Mesh
from jax.sharding import PartitionSpec as P

ROW = ("y", "zl", "core")
COL = ("zh", "x")
bf16, f32 = jnp.bfloat16, jnp.float32
tie = lax.optimization_barrier


def gelu_parts(pre):
    scale_c = math.sqrt(2.0 / math.pi)
    inner = jnp.tanh(scale_c * (pre + 0.044715 * pre * pre * pre))
    active = 0.5 * pre * (1.0 + inner)
    slope = 0.5 * (1.0 + inner) + 0.5 * pre * (1.0 - inner * inner) * scale_c * (
        1.0 + 3.0 * 0.044715 * pre * pre
    )
    return (active, slope)


def shift(v, axis, by, size=4):
    return lax.ppermute(v, axis, [(i, (i + by) % size) for i in range(size)])


def ring_first(v, axis):
    return shift(v, axis, 1), shift(v, axis, -1)


def ring_second(v, before, after, axis):
    half = v.shape[0] // 2
    far = jnp.concatenate([shift(before[:half], axis, 1), shift(after[half:], axis, -1)])
    return [v, after, far, before]


def pair(first, mine, other):
    return jnp.where(first, mine, other), jnp.where(first, other, mine)


def spread(part, zl):
    n = part.shape[0] // 4

    def block(r):
        return lax.dynamic_slice_in_dim(part, (zl + r) % 4 * n, n, 0)

    total = block(0)
    for r in (1, 3, 2):
        total = total + shift(block(r).astype(bf16), "zl", r).astype(f32)
    return total


def dot_t(a, b):
    return lax.dot_general(a, b, (((0,), (0,)), ((), ())), preferred_element_type=f32)


def body(tokens_in, out_grad, pre_act, w_down):
    y, zl, core, zh, x = (lax.axis_index(a) for a in ("y", "zl", "core", "zh", "x"))
    first = core == 0
    kd, full = w_down.shape
    kt = pre_act.shape[0]
    half = full // 2
    chip = 2 * kd
    w_all = lax.all_gather(w_down, ROW, axis=0, tiled=True)

    with jax.named_scope("swap_pre"):
        low, high = pre_act[:, :half], pre_act[:, half:]
        mine, theirs = jnp.where(first, low, high), jnp.where(first, high, low)
        pre = jnp.concatenate(pair(first, mine, shift(theirs, "core", 1, 2)))
    with jax.named_scope("quarter"):
        perms = ([], [], [], [])
        for yy in range(4):
            for hh in range(2):
                for xx in range(4):
                    dst = (yy * 2 + hh) * 4 + xx
                    for k in range(2):
                        qq = (xx + yy) % 4
                        perms[k].append(((yy * 2 + qq // 2) * 4 + 2 * (qq % 2) + (hh + k) % 2, dst))
                        src = ((yy - xx) % 4 * 2 + yy // 2) * 4 + 2 * (yy % 2) + (hh + k) % 2
                        perms[2 + k].append((src, dst))
        r = [lax.ppermute(out_grad, ("y", "zh", "x"), p) for p in perms]
        q = (x + y) % 4
        quarter = 2 * out_grad.shape[0]
        tok_q = lax.dynamic_slice_in_dim(tokens_in, q * quarter, quarter, 0)
        og_q = [jnp.concatenate([jnp.where(zh == 0, a, b), jnp.where(zh == 0, b, a)]) for a, b in (r[:2], r[2:])]
    active, slope = gelu_parts(pre.astype(f32))
    act = active.astype(bf16)
    with jax.named_scope("og_swap"):
        three = jnp.stack([tok_q] + og_q).reshape(3, 4, 2, kt, kd)
        mine = jnp.where(first, three[:, :, 0], three[:, :, 1])
        theirs = jnp.where(first, three[:, :, 1], three[:, :, 0])
        lo, hi = pair(first, mine, shift(theirs, "core", 1, 2))
        three = jnp.concatenate([lo, hi], -1)
    with jax.named_scope("og_zl"):
        got = [lax.dynamic_index_in_dim(three, (zl - r) % 4, 1, False) for r in range(4)]
        got = [got[0]] + [shift(got[r], "zl", -r) for r in range(1, 4)]
        got = jnp.stack(got + got)
        got = lax.dynamic_slice_in_dim(got, (4 - zl) % 4, 4, 0)
        three = jnp.concatenate([got[k] for k in range(4)], -1)
    with jax.named_scope("act_y"):
        b0, a0 = ring_first(act, "y")
        act_all = jnp.concatenate(ring_second(act, b0, a0, "y"))
    with jax.named_scope("og_x"):
        flat = three.reshape(-1, 4 * chip)
        b3, a3 = ring_first(flat, "x")
        slots = ring_second(flat, b3, a3, "x")
    with jax.named_scope("og_core"):
        buf = jnp.zeros((12, kt, 4 * chip), bf16)
        for r in range(4):
            v = slots[r].reshape(3, kt, 4 * chip)
            for k in range(2):
                buf = lax.dynamic_update_slice_in_dim(buf, v[k : k + 1], 4 * k + (x + r) % 4, 0)
            buf = lax.dynamic_update_slice_in_dim(buf, v[2:], 8 + (y - x - r) % 4, 0)
        buf = jnp.concatenate(pair(first, buf, shift(buf, "core", 1, 2)), 1)
        tok = buf[:4].reshape(-1, 4 * chip)
        og = buf[4:8].reshape(-1, 4 * chip)

    with jax.named_scope("down"):
        down = spread(dot_t(og, act_all), zl)

    with jax.named_scope("hid"):
        w_half = lax.dynamic_slice_in_dim(w_all, core * half, half, 1)
        hid = None
        for r in range(4):
            term = jnp.dot(buf[8 + r], w_half[r * 4 * chip : (r + 1) * 4 * chip], preferred_element_type=f32)
            hid = term if hid is None else hid + term
        pre_grad = (hid * slope).astype(bf16)
    with jax.named_scope("grad_y"):
        bb, aa = ring_first(pre_grad, "y")
        grad_all = jnp.concatenate(ring_second(pre_grad, bb, aa, "y"))
    with jax.named_scope("up"):
        up = spread(dot_t(tok, grad_all), zl)

    outs = []
    with jax.named_scope("swap_out"):
        for total in (up, down):
            a, b = total[:kd], total[kd:]
            mine, theirs = jnp.where(first, a, b), jnp.where(first, b, a)
            outs.append(jnp.concatenate(pair(first, mine, shift(theirs, "core", 1, 2)), 1))
    return tuple(outs)


def solution(mesh):
    fine = Mesh(mesh.devices.reshape(4, 4, 2, 2, 4), ROW + COL)
    return jax.shard_map(
        body,
        mesh=fine,
        in_specs=(P(None, ROW), P(COL, ROW), P(ROW, COL), P(ROW, COL)),
        out_specs=(P(ROW, COL), P(ROW, COL)),
        check_vma=False,
    )
```

```python
import math

import jax
import jax.numpy as jnp
from jax import lax
from jax.sharding import Mesh
from jax.sharding import PartitionSpec as P

ROW = ("y", "zl", "core")
COL = ("zh", "x")
bf16, f32 = jnp.bfloat16, jnp.float32
tie = lax.optimization_barrier


def gelu_parts(pre):
    scale_c = math.sqrt(2.0 / math.pi)
    inner = jnp.tanh(scale_c * (pre + 0.044715 * pre * pre * pre))
    active = 0.5 * pre * (1.0 + inner)
    slope = 0.5 * (1.0 + inner) + 0.5 * pre * (1.0 - inner * inner) * scale_c * (
        1.0 + 3.0 * 0.044715 * pre * pre
    )
    return (active, slope)


def shift(v, axis, by, size=4):
    return lax.ppermute(v, axis, [(i, (i + by) % size) for i in range(size)])


def ring_first(v, axis):
    return shift(v, axis, 1), shift(v, axis, -1)


def ring_second(v, before, after, axis):
    half = v.shape[0] // 2
    far = jnp.concatenate([shift(before[:half], axis, 1), shift(after[half:], axis, -1)])
    return [v, after, far, before]


def pair(first, mine, other):
    return jnp.where(first, mine, other), jnp.where(first, other, mine)


def cut(part, zl):
    n = part.shape[0] // 4

    def block(r):
        return lax.dynamic_slice_in_dim(part, (zl + r) % 4 * n, n, 0)

    return block(0), [block(r).astype(bf16) for r in (1, 3, 2)]


def spread(blocks):
    return [shift(b, "zl", r) for b, r in zip(blocks, (1, 3, 2))]


def total_of(own, others):
    for o in others:
        own = own + o.astype(f32)
    return own


def dot_t(a, b):
    return lax.dot_general(a, b, (((0,), (0,)), ((), ())), preferred_element_type=f32)


def body(tokens_in, out_grad, pre_act, w_down):
    y, zl, core, zh, x = (lax.axis_index(a) for a in ("y", "zl", "core", "zh", "x"))
    first = core == 0
    kd, full = w_down.shape
    kt = pre_act.shape[0]
    half = full // 2
    chip = 2 * kd
    w_all = lax.all_gather(w_down, ROW, axis=0, tiled=True)

    with jax.named_scope("swap_pre"):
        low, high = pre_act[:, :half], pre_act[:, half:]
        mine, theirs = jnp.where(first, low, high), jnp.where(first, high, low)
        pre = jnp.concatenate([mine, shift(theirs, "core", 1, 2)])
    with jax.named_scope("quarter"):
        perms = ([], [], [], [])
        for yy in range(4):
            for hh in range(2):
                for xx in range(4):
                    dst = (yy * 2 + hh) * 4 + xx
                    for k in range(2):
                        qq = (xx + yy) % 4
                        perms[k].append(((yy * 2 + qq // 2) * 4 + 2 * (qq % 2) + (hh + k) % 2, dst))
                        src = ((yy - xx) % 4 * 2 + yy // 2) * 4 + 2 * (yy % 2) + (hh + k) % 2
                        perms[2 + k].append((src, dst))
        r = [lax.ppermute(out_grad, ("y", "zh", "x"), p) for p in perms]
        q = (x + y) % 4
        quarter = 2 * out_grad.shape[0]
        tok_q = lax.dynamic_slice_in_dim(tokens_in, q * quarter, quarter, 0)
        og_q = [jnp.concatenate([jnp.where(zh == 0, a, b), jnp.where(zh == 0, b, a)]) for a, b in (r[:2], r[2:])]
    og_q[0], og_q[1], pre = tie((og_q[0], og_q[1], pre))
    active, slope = gelu_parts(pre.astype(f32))
    act = active.astype(bf16)
    with jax.named_scope("act_y"):
        b0, a0 = ring_first(act, "y")
    with jax.named_scope("og_swap"):
        three = jnp.stack([tok_q] + og_q).reshape(3, 4, 2, kt, kd)
        mine = jnp.where(first, three[:, :, 0], three[:, :, 1])
        theirs = jnp.where(first, three[:, :, 1], three[:, :, 0])
        lo, hi = pair(first, mine, shift(theirs, "core", 1, 2))
        three = jnp.concatenate([lo, hi], -1)
    with jax.named_scope("og_zl"):
        got = [lax.dynamic_index_in_dim(three, (zl - r) % 4, 1, False) for r in range(4)]
        got = [got[0]] + [shift(got[r], "zl", -r) for r in range(1, 4)]
        got, b0, a0 = tie((got, b0, a0))
        got = jnp.stack(got + got)
        got = lax.dynamic_slice_in_dim(got, (4 - zl) % 4, 4, 0)
        three = jnp.concatenate([got[k] for k in range(4)], -1)
    with jax.named_scope("act_y2"):
        act_all = jnp.concatenate(ring_second(act, b0, a0, "y"))
    with jax.named_scope("og_x"):
        flat = three.reshape(-1, 4 * chip)
        b3, a3 = ring_first(flat, "x")
        b3, a3, act_all = tie((b3, a3, act_all))
        slots = ring_second(flat, b3, a3, "x")
    with jax.named_scope("og_core"):
        buf = jnp.zeros((12, kt, 4 * chip), bf16)
        for r in range(4):
            v = slots[r].reshape(3, kt, 4 * chip)
            for k in range(2):
                buf = lax.dynamic_update_slice_in_dim(buf, v[k : k + 1], 4 * k + (x + r) % 4, 0)
            buf = lax.dynamic_update_slice_in_dim(buf, v[2:], 8 + (y - x - r) % 4, 0)
        tok, og = buf[:4], buf[4:]
        tok = jnp.concatenate([tok, shift(tok, "core", 1, 2)], 1).reshape(-1, 4 * chip)
        og = jnp.concatenate([og, shift(og, "core", 1, 2)], 1)

    with jax.named_scope("down"):
        own, blocks = cut(dot_t(og[:4].reshape(-1, 4 * chip), act_all), zl)
        og, own, blocks = tie((og, own, blocks))
        down = spread(blocks)

    with jax.named_scope("hid"):
        w_half = lax.dynamic_slice_in_dim(w_all, core * half, half, 1)
        hid = None
        for r in range(4):
            term = jnp.dot(og[4 + r], w_half[r * 4 * chip : (r + 1) * 4 * chip], preferred_element_type=f32)
            hid = term if hid is None else hid + term
        pre_grad = (hid * slope).astype(bf16)
    with jax.named_scope("grad_y"):
        bb, aa = ring_first(pre_grad, "y")
        bb, aa, down[0], down[1] = tie((bb, aa, down[0], down[1]))
        grad_all = jnp.concatenate(ring_second(pre_grad, bb, aa, "y"))
    with jax.named_scope("up"):
        grad_all, down = tie((grad_all, down))
        down = total_of(own, down)
        own, blocks = cut(dot_t(tok, grad_all), zl)
        up = total_of(own, spread(blocks))

    outs = []
    with jax.named_scope("swap_out"):
        for total in (up, down):
            a, b = total[:kd], total[kd:]
            mine, theirs = jnp.where(first, a, b), jnp.where(first, b, a)
            outs.append(jnp.concatenate(pair(first, mine, shift(theirs, "core", 1, 2)), 1))
    return tuple(outs)


def solution(mesh):
    fine = Mesh(mesh.devices.reshape(4, 4, 2, 2, 4), ROW + COL)
    return jax.shard_map(
        body,
        mesh=fine,
        in_specs=(P(None, ROW), P(COL, ROW), P(ROW, COL), P(ROW, COL)),
        out_specs=(P(ROW, COL), P(ROW, COL)),
        check_vma=False,
    )
```

```python
import math

import jax
import jax.numpy as jnp
from jax import lax
from jax.sharding import Mesh
from jax.sharding import PartitionSpec as P

ROW = ("y", "zl", "core")
COL = ("zh", "x")
bf16, f32 = jnp.bfloat16, jnp.float32
tie = lax.optimization_barrier


def gelu_parts(pre):
    scale_c = math.sqrt(2.0 / math.pi)
    inner = jnp.tanh(scale_c * (pre + 0.044715 * pre * pre * pre))
    active = 0.5 * pre * (1.0 + inner)
    slope = 0.5 * (1.0 + inner) + 0.5 * pre * (1.0 - inner * inner) * scale_c * (
        1.0 + 3.0 * 0.044715 * pre * pre
    )
    return (active, slope)


def shift(v, axis, by, size=4):
    return lax.ppermute(v, axis, [(i, (i + by) % size) for i in range(size)])


def ring_first(v, axis):
    return shift(v, axis, 1), shift(v, axis, -1)


def ring_second(v, before, after, axis):
    half = v.shape[0] // 2
    far = jnp.concatenate([shift(before[:half], axis, 1), shift(after[half:], axis, -1)])
    return [v, after, far, before]


def turned(slots, by):
    def pick(k):
        i = (k + by) % 4
        return jnp.where(i < 2, jnp.where(i == 0, slots[0], slots[1]), jnp.where(i == 2, slots[2], slots[3]))

    return [pick(k) for k in range(4)]


def dot_t(a, b):
    return lax.dot_general(a, b, (((0,), (0,)), ((), ())), preferred_element_type=f32)


def product(own, other, right):
    theirs = shift(dot_t(other, right), "core", 1, 2)
    mine, theirs = tie((dot_t(own, right), theirs))
    total = mine + theirs
    n = total.shape[0] // 4
    return [total[r * n : (r + 1) * n] for r in range(4)]


def spread(blocks):
    return [shift(blocks[r].astype(bf16), "zl", r) for r in (1, 3, 2)]


def total_of(own, others):
    for o in others:
        own = own + o.astype(f32)
    return own


def body(tokens_in, out_grad, pre_act, w_down):
    y, zl, core, zh, x = (lax.axis_index(a) for a in ("y", "zl", "core", "zh", "x"))
    first = core == 0
    kd, full = w_down.shape
    kt = pre_act.shape[0]
    w_all = lax.all_gather(w_down, ROW, axis=0, tiled=True)

    with jax.named_scope("quarter"):
        perms = ([], [], [], [])
        for yy in range(4):
            for hh in range(2):
                for xx in range(4):
                    dst = (yy * 2 + hh) * 4 + xx
                    for k in range(2):
                        qq = (xx + yy) % 4
                        perms[k].append(((yy * 2 + qq // 2) * 4 + 2 * (qq % 2) + (hh + k) % 2, dst))
                        src = ((yy - xx) % 4 * 2 + yy // 2) * 4 + 2 * (yy % 2) + (hh + k) % 2
                        perms[2 + k].append((src, dst))
        r = [lax.ppermute(out_grad, ("y", "zh", "x"), p) for p in perms]
        q = (x + y) % 4
        quarter = 2 * out_grad.shape[0]
        tok_q = lax.dynamic_slice_in_dim(tokens_in, q * quarter, quarter, 0)
        og_q = [jnp.concatenate([jnp.where(zh == 0, a, b), jnp.where(zh == 0, b, a)]) for a, b in (r[:2], r[2:])]
    active, slope = gelu_parts(pre_act.astype(f32))
    act = active.astype(bf16)
    og_q[0], og_q[1], act = tie((og_q[0], og_q[1], act))
    with jax.named_scope("act_y"):
        b0, a0 = ring_first(act, "y")
    with jax.named_scope("og_swap"):
        three = jnp.stack([tok_q] + og_q).reshape(3, 4, 2, kt, kd)
        mine = jnp.where(first, three[:, :, 0], three[:, :, 1])
        theirs = jnp.where(first, three[:, :, 1], three[:, :, 0])
        theirs = shift(theirs, "core", 1, 2)
        three = jnp.concatenate([mine, theirs], -1)
    with jax.named_scope("og_zl"):
        got = [lax.dynamic_index_in_dim(three, (zl - r) % 4, 1, False) for r in range(4)]
        got = [got[0]] + [shift(got[r], "zl", -r) for r in range(1, 4)]
        got, b0, a0 = tie((got, b0, a0))
        tok, og = (jnp.concatenate([g[k, :, c : c + kd] for c in (0, kd) for g in got], 1) for k in (0, 1))
        swapped = [jnp.where(first, g[2], jnp.concatenate([g[2, :, kd:], g[2, :, :kd]], 1)) for g in got]
        og_h = jnp.concatenate(turned(swapped, -zl), 1)
    with jax.named_scope("act_y2"):
        act_all = jnp.concatenate(ring_second(act, b0, a0, "y"))
    with jax.named_scope("og_x"):
        flat = jnp.concatenate([og, og_h])
        b3, a3 = ring_first(flat, "x")
        b3, a3, act_all = tie((b3, a3, act_all))
        slots = ring_second(flat, b3, a3, "x")
        og = jnp.concatenate(turned([s[:kt] for s in slots], -x))
        og_h = jnp.concatenate(turned([s[kt:] for s in slots[:1] + slots[:0:-1]], x - y), 1)
    half = 4 * kd

    with jax.named_scope("down"):
        blocks = product(og[:, :half], og[:, half:], act_all)
        og_h, blocks = tie((og_h, blocks))
        parts = spread(blocks)
    with jax.named_scope("hid"):
        hid = jnp.dot(og_h, w_all, preferred_element_type=f32)
        pre_grad = (hid * slope).astype(bf16)
    with jax.named_scope("grad_y"):
        pre_grad, parts[0], tok = tie((pre_grad, parts[0], tok))
        bb, aa = ring_first(pre_grad, "y")
    with jax.named_scope("tok_x"):
        b4, a4 = ring_first(tok, "x")
        tok = jnp.concatenate(turned(ring_second(tok, b4, a4, "x"), -x))
    with jax.named_scope("grad_y"):
        bb, aa, parts[1] = tie((bb, aa, parts[1]))
        grad_all = jnp.concatenate(ring_second(pre_grad, bb, aa, "y"))
        grad_all, parts[2] = tie((grad_all, parts[2]))
        down = total_of(blocks[0], parts)
    with jax.named_scope("up"):
        blocks = product(tok[:, :half], tok[:, half:], grad_all)
        up = total_of(blocks[0], spread(blocks))
    return (up, down)


def solution(mesh):
    fine = Mesh(mesh.devices.reshape(4, 4, 2, 2, 4), ROW + COL)
    return jax.shard_map(
        body,
        mesh=fine,
        in_specs=(P(None, ROW), P(COL, ROW), P(ROW, COL), P(ROW, COL)),
        out_specs=(P(ROW, COL), P(ROW, COL)),
        check_vma=False,
    )
```

```python
import math

import jax
import jax.numpy as jnp
from jax import lax
from jax.sharding import Mesh
from jax.sharding import PartitionSpec as P

ROW = ("y", "zl", "core")
COL = ("zh", "x")
bf16, f32 = jnp.bfloat16, jnp.float32
tie = lax.optimization_barrier


def gelu_parts(pre):
    scale_c = math.sqrt(2.0 / math.pi)
    inner = jnp.tanh(scale_c * (pre + 0.044715 * pre * pre * pre))
    active = 0.5 * pre * (1.0 + inner)
    slope = 0.5 * (1.0 + inner) + 0.5 * pre * (1.0 - inner * inner) * scale_c * (
        1.0 + 3.0 * 0.044715 * pre * pre
    )
    return (active, slope)


def shift(v, axis, by, size=4):
    return lax.ppermute(v, axis, [(i, (i + by) % size) for i in range(size)])


def ring_first(v, axis):
    return shift(v, axis, 1), shift(v, axis, -1)


def ring_second(v, before, after, axis):
    half = v.shape[0] // 2
    far = jnp.concatenate([shift(before[:half], axis, 1), shift(after[half:], axis, -1)])
    return [v, after, far, before]


def turned(slots, by):
    def pick(k):
        i = (k + by) % 4
        return jnp.where(i < 2, jnp.where(i == 0, slots[0], slots[1]), jnp.where(i == 2, slots[2], slots[3]))

    return [pick(k) for k in range(4)]


def dot_t(a, b):
    return lax.dot_general(a, b, (((0,), (0,)), ((), ())), preferred_element_type=f32)


def product(own, other, right):
    theirs = shift(dot_t(other, right), "core", 1, 2)
    mine, theirs = tie((dot_t(own, right), theirs))
    total = mine + theirs
    n = total.shape[0] // 4
    return [total[r * n : (r + 1) * n] for r in range(4)]


def spread(blocks):
    return [shift(blocks[r].astype(bf16), "zl", r) for r in (1, 3, 2)]


def total_of(own, others):
    for o in others:
        own = own + o.astype(f32)
    return own


def body(tokens_in, out_grad, pre_act, w_down):
    y, zl, core, zh, x = (lax.axis_index(a) for a in ("y", "zl", "core", "zh", "x"))
    first = core == 0
    kd, full = w_down.shape
    kt = pre_act.shape[0]
    w_all = lax.all_gather(w_down, ROW, axis=0, tiled=True)

    quarter = 2 * out_grad.shape[0]
    perms = ([], [], [], [])
    for yy in range(4):
        for hh in range(2):
            for xx in range(4):
                dst = (yy * 2 + hh) * 4 + xx
                for k in range(2):
                    src = ((yy - xx) % 4 * 2 + yy // 2) * 4 + 2 * (yy % 2) + (hh + k) % 2
                    perms[k].append((src, dst))
                    qq = (xx + yy) % 4
                    perms[2 + k].append(((yy * 2 + qq // 2) * 4 + 2 * (qq % 2) + (hh + k) % 2, dst))

    def ordered(a, b):
        return jnp.concatenate([jnp.where(zh == 0, a, b), jnp.where(zh == 0, b, a)])

    def both_cores(v):
        v = v.reshape(v.shape[:-2] + (4, 2, kt, kd))
        mine = jnp.where(first, v[..., 0, :, :], v[..., 1, :, :])
        theirs = jnp.where(first, v[..., 1, :, :], v[..., 0, :, :])
        return jnp.concatenate([mine, shift(theirs, "core", 1, 2)], -1)

    def along_zl(v, axis):
        got = [lax.dynamic_index_in_dim(v, (zl - r) % 4, axis, False) for r in range(4)]
        return [got[0]] + [shift(got[r], "zl", -r) for r in range(1, 4)]

    with jax.named_scope("hid_quarter"):
        r0, r1 = (lax.ppermute(out_grad, ("y", "zh", "x"), p) for p in perms[:2])
        r0, r1, out_grad = tie((r0, r1, out_grad))
    active, slope = gelu_parts(pre_act.astype(f32))
    act = active.astype(bf16)
    with jax.named_scope("hid_core"):
        og_h = both_cores(ordered(r0, r1))
    with jax.named_scope("quarter"):
        r2, r3 = (lax.ppermute(out_grad, ("y", "zh", "x"), p) for p in perms[2:])
    with jax.named_scope("hid_zl"):
        got = along_zl(og_h, 0)
        got, r2, r3, act = tie((got, r2, r3, act))
        swapped = [jnp.where(first, g, jnp.concatenate([g[:, kd:], g[:, :kd]], 1)) for g in got]
        og_h = jnp.concatenate(turned(swapped, -zl), 1)
    with jax.named_scope("hid_x"):
        b3, a3 = ring_first(og_h, "x")
    with jax.named_scope("two_core"):
        tok_q = lax.dynamic_slice_in_dim(tokens_in, (x + y) % 4 * quarter, quarter, 0)
        two = both_cores(jnp.stack([tok_q, ordered(r2, r3)]))
        b3, a3, two = tie((b3, a3, two))
    with jax.named_scope("hid_x2"):
        slots = ring_second(og_h, b3, a3, "x")
    with jax.named_scope("act_y"):
        b0, a0 = ring_first(act, "y")
    with jax.named_scope("two_zl"):
        got = along_zl(two, 1)
        slots, got, b0, a0 = tie((slots, got, b0, a0))
        og_h = jnp.concatenate(turned(slots[:1] + slots[:0:-1], x - y), 1)
        two = jnp.concatenate([jnp.concatenate([g[k, :, c : c + kd] for c in (0, kd) for g in got], 1) for k in (0, 1)])
    with jax.named_scope("hid"):
        hid = jnp.dot(og_h, w_all, preferred_element_type=f32)
        pre_grad = (hid * slope).astype(bf16)
    with jax.named_scope("act_y2"):
        act_all = jnp.concatenate(ring_second(act, b0, a0, "y"))
    with jax.named_scope("two_x"):
        b4, a4 = ring_first(two, "x")
        b4, a4, act_all, pre_grad = tie((b4, a4, act_all, pre_grad))
        slots = ring_second(two, b4, a4, "x")
    with jax.named_scope("grad_y"):
        bb, aa = ring_first(pre_grad, "y")
        bb, aa, slots = tie((bb, aa, slots))
    half = 4 * kd
    with jax.named_scope("down"):
        tok, og = (jnp.concatenate(turned([s[k : k + kt] for s in slots], -x)) for k in (0, kt))
        blocks = product(og[:, :half], og[:, half:], act_all)
        parts = spread(blocks)
    with jax.named_scope("grad_y2"):
        grad_all = jnp.concatenate(ring_second(pre_grad, bb, aa, "y"))
        grad_all, blocks, parts[0] = tie((grad_all, blocks, parts[0]))
    with jax.named_scope("up"):
        up_blocks = product(tok[:, :half], tok[:, half:], grad_all)
        up_blocks, parts[1] = tie((up_blocks, parts[1]))
        up = total_of(up_blocks[0], spread(up_blocks))
    return (up, total_of(blocks[0], parts))


def solution(mesh):
    fine = Mesh(mesh.devices.reshape(4, 4, 2, 2, 4), ROW + COL)
    return jax.shard_map(
        body,
        mesh=fine,
        in_specs=(P(None, ROW), P(COL, ROW), P(ROW, COL), P(ROW, COL)),
        out_specs=(P(ROW, COL), P(ROW, COL)),
        check_vma=False,
    )
```

```python
import math

import jax
import jax.numpy as jnp
from jax import lax
from jax.sharding import Mesh
from jax.sharding import PartitionSpec as P

ROW = ("y", "zl", "core")
COL = ("zh", "x")
bf16, f32 = jnp.bfloat16, jnp.float32
tie = lax.optimization_barrier


def gelu_parts(pre):
    scale_c = math.sqrt(2.0 / math.pi)
    inner = jnp.tanh(scale_c * (pre + 0.044715 * pre * pre * pre))
    active = 0.5 * pre * (1.0 + inner)
    slope = 0.5 * (1.0 + inner) + 0.5 * pre * (1.0 - inner * inner) * scale_c * (
        1.0 + 3.0 * 0.044715 * pre * pre
    )
    return (active, slope)


def shift(v, axis, by, size=4):
    return lax.ppermute(v, axis, [(i, (i + by) % size) for i in range(size)])


def ring_first(v, axis):
    return shift(v, axis, 1), shift(v, axis, -1)


def ring_second(v, before, after, axis):
    half = v.shape[0] // 2
    far = jnp.concatenate([shift(before[:half], axis, 1), shift(after[half:], axis, -1)])
    return [v, after, far, before]


def turned(slots, by):
    def pick(k):
        i = (k + by) % 4
        return jnp.where(i < 2, jnp.where(i == 0, slots[0], slots[1]), jnp.where(i == 2, slots[2], slots[3]))

    return [pick(k) for k in range(4)]


def dot_t(a, b):
    return lax.dot_general(a, b, (((0,), (0,)), ((), ())), preferred_element_type=f32)


def body(tokens_in, out_grad, pre_act, w_down):
    y, zl, core, zh, x = (lax.axis_index(a) for a in ("y", "zl", "core", "zh", "x"))
    first = core == 0
    kd, full = w_down.shape
    kt = pre_act.shape[0]
    nf = full // 4
    nd = 4 * kd
    nt = 4 * kt
    quarter = 2 * out_grad.shape[0]

    with jax.named_scope("units_zl"):
        rows = jnp.concatenate([w_down, pre_act])
        wp = [lax.dynamic_slice_in_dim(rows, (zl - r) % 4 * nf, nf, 1) for r in range(4)]
        wp = [wp[0]] + [shift(wp[r], "zl", -r) for r in range(1, 4)]
    with jax.named_scope("tok_turn"):
        moves = [(yy * 4 + xx, (yy + xx) % 4 * 4 + xx) for yy in range(4) for xx in range(4)]
        tok = lax.dynamic_slice_in_dim(tokens_in, (y + x) % 4 * quarter, quarter, 0)
        tok = lax.ppermute(tok, ("y", "x"), moves)
    with jax.named_scope("og_turn"):
        perms = ([], [])
        for yy in range(4):
            for hh in range(2):
                for xx in range(4):
                    for k in range(2):
                        src = ((yy - xx) % 4 * 2 + yy // 2) * 4 + 2 * (yy % 2) + (hh + k) % 2
                        perms[k].append((src, (yy * 2 + hh) * 4 + xx))
        r0, r1 = (lax.ppermute(out_grad, ("y", "zh", "x"), p) for p in perms)
    wp, tok, r0, r1 = tie((wp, tok, r0, r1))

    with jax.named_scope("core"):
        og = jnp.concatenate([jnp.where(zh == 0, r0, r1), jnp.where(zh == 0, r1, r0)])
        two = jnp.stack([tok, og]).reshape(2, 4, 2, kt, kd)
        mine = jnp.where(first, two[:, :, 0], two[:, :, 1])
        theirs = jnp.where(first, two[:, :, 1], two[:, :, 0])
        two = jnp.concatenate([mine, shift(theirs, "core", 1, 2)], -1).reshape(2, nt, 2 * kd)

    def along_zl(v):
        got = [v] + [shift(v, "zl", -r) for r in range(1, 4)]
        return got

    def features(got):
        return jnp.concatenate([g[:, c : c + kd] for c in (0, kd) for g in got], 1)

    with jax.named_scope("tok_zl"):
        got_t = along_zl(two[0])
    with jax.named_scope("w_y"):
        w_own = jnp.concatenate([v[:kd] for v in wp])
        b1, a1 = ring_first(w_own, "y")
        got_t, b1, a1, og = tie((got_t, b1, a1, two[1]))
    with jax.named_scope("og_zl"):
        got_o = along_zl(og)
    with jax.named_scope("tok_x"):
        tok = features(got_t)
        b2, a2 = ring_first(tok, "x")
    with jax.named_scope("w_y2"):
        w_all = jnp.concatenate(ring_second(w_own, b1, a1, "y"))
    b2, a2, got_o, w_all = tie((b2, a2, got_o, w_all))
    with jax.named_scope("tok_x2"):
        toks = ring_second(tok, b2, a2, "x")
    with jax.named_scope("og_x"):
        og = features(got_o)
        b3, a3 = ring_first(og, "x")
    with jax.named_scope("w_core"):
        w_all = [v.reshape(4, nd, nf) for v in (w_all, shift(w_all, "core", 1, 2))]
        w_all = [jnp.concatenate(v) for v in zip(*(turned([u[0], u[3], u[2], u[1]], x) for u in w_all))]
        pre = jnp.concatenate(turned([v[kd:] for v in wp], -zl)).astype(f32)
        active, slope = gelu_parts(pre)
        act = active.astype(bf16)
        toks, b3, a3, w_all, act, slope = tie((toks, b3, a3, w_all, act, slope))
    with jax.named_scope("og_x2"):
        ogs = ring_second(og, b3, a3, "x")

    def theirs_of(slots, right):
        return dot_t(jnp.concatenate([s[:, nd:] for s in slots], 1), right)

    def mine_of(slots, right):
        return dot_t(jnp.concatenate([s[:, :nd] for s in slots], 1), right)

    with jax.named_scope("down"):
        other = theirs_of(ogs, act)
        ogs, other = tie((ogs, other))
        other = shift(other, "core", 1, 2)
    with jax.named_scope("hid"):
        hid = None
        for s in range(4):
            term = jnp.dot(ogs[s], w_all[s], preferred_element_type=f32)
            hid = term if hid is None else hid + term
        pre_grad = (hid * slope).astype(bf16)
    with jax.named_scope("up"):
        up_other = theirs_of(toks, pre_grad)
        up_other, ogs = tie((up_other, ogs))
        up_other = shift(up_other, "core", 1, 2)
    mine = tie((mine_of(ogs, act), mine_of(toks, pre_grad)))
    down, up = mine[0] + other, mine[1] + up_other
    with jax.named_scope("sum_y"):
        blocks = [[lax.dynamic_slice_in_dim(v, (-x - r) % 4 * nd, nd, 0) for r in range(4)] for v in (down, up)]
        (d0, d1, d2, d3), (u0, u1, u2, u3) = blocks
        fd, fu = shift(d2.astype(bf16), "y", 1), shift(u2.astype(bf16), "y", -1)
        before = shift(jnp.concatenate([d1 + fd.astype(f32), u1]).astype(bf16), "y", 1)
        after = shift(jnp.concatenate([d3, u3 + fu.astype(f32)]).astype(bf16), "y", -1)
        total = jnp.concatenate([d0, u0]) + before.astype(f32) + after.astype(f32)
    with jax.named_scope("place"):
        total = total.reshape(2, 4, kd, nf)
        outs = [total[:, 0]] + [shift(total[:, r].astype(bf16), "zl", r).astype(f32) for r in (3, 2, 1)]
        out = jnp.concatenate(turned(outs, -zl), -1)
    return (out[1], out[0])


def solution(mesh):
    fine = Mesh(mesh.devices.reshape(4, 4, 2, 2, 4), ROW + COL)
    return jax.shard_map(
        body,
        mesh=fine,
        in_specs=(P(None, ROW), P(COL, ROW), P(ROW, COL), P(ROW, COL)),
        out_specs=(P(ROW, COL), P(ROW, COL)),
        check_vma=False,
    )
```

```python
import math

import jax
import jax.numpy as jnp
from jax import lax
from jax.sharding import Mesh
from jax.sharding import PartitionSpec as P

ROW = ("y", "zl", "core")
COL = ("zh", "x")
bf16, f32 = jnp.bfloat16, jnp.float32
tie = lax.optimization_barrier


def gelu_parts(pre):
    scale_c = math.sqrt(2.0 / math.pi)
    inner = jnp.tanh(scale_c * (pre + 0.044715 * pre * pre * pre))
    active = 0.5 * pre * (1.0 + inner)
    slope = 0.5 * (1.0 + inner) + 0.5 * pre * (1.0 - inner * inner) * scale_c * (
        1.0 + 3.0 * 0.044715 * pre * pre
    )
    return (active, slope)


def shift(v, axis, by, size=4):
    return lax.ppermute(v, axis, [(i, (i + by) % size) for i in range(size)])


def ring_first(v, axis):
    return shift(v, axis, 1), shift(v, axis, -1)


def ring_second(v, before, after, axis):
    half = v.shape[0] // 2
    far = jnp.concatenate([shift(before[:half], axis, 1), shift(after[half:], axis, -1)])
    return [v, after, far, before]


def turned(slots, by):
    def pick(k):
        i = (k + by) % 4
        return jnp.where(i < 2, jnp.where(i == 0, slots[0], slots[1]), jnp.where(i == 2, slots[2], slots[3]))

    return [pick(k) for k in range(4)]


def dot_t(a, b):
    return lax.dot_general(a, b, (((0,), (0,)), ((), ())), preferred_element_type=f32)


def product(own, other, right):
    theirs = shift(dot_t(other, right), "core", 1, 2)
    mine, theirs = tie((dot_t(own, right), theirs))
    total = mine + theirs
    n = total.shape[0] // 4
    return [total[r * n : (r + 1) * n] for r in range(4)]


def spread(blocks):
    return [shift(blocks[r].astype(bf16), "zl", r) for r in (1, 3, 2)]


def total_of(own, others):
    for o in others:
        own = own + o.astype(f32)
    return own


def body(tokens_in, out_grad, pre_act, w_down):
    y, zl, core, zh, x = (lax.axis_index(a) for a in ("y", "zl", "core", "zh", "x"))
    first = core == 0
    kd, full = w_down.shape
    kt = pre_act.shape[0]
    part = full // 2
    w_all = [lax.all_gather(w_down[:, k * part : (k + 1) * part], ROW, axis=0, tiled=True) for k in range(2)]

    with jax.named_scope("quarter"):
        perms = ([], [], [], [])
        for yy in range(4):
            for hh in range(2):
                for xx in range(4):
                    dst = (yy * 2 + hh) * 4 + xx
                    for k in range(2):
                        qq = (xx + yy) % 4
                        perms[k].append(((yy * 2 + qq // 2) * 4 + 2 * (qq % 2) + (hh + k) % 2, dst))
                        src = ((yy - xx) % 4 * 2 + yy // 2) * 4 + 2 * (yy % 2) + (hh + k) % 2
                        perms[2 + k].append((src, dst))
        r = [lax.ppermute(out_grad, ("y", "zh", "x"), p) for p in perms]
        q = (x + y) % 4
        quarter = 2 * out_grad.shape[0]
        tok_q = lax.dynamic_slice_in_dim(tokens_in, q * quarter, quarter, 0)
        og_q = [jnp.concatenate([jnp.where(zh == 0, a, b), jnp.where(zh == 0, b, a)]) for a, b in (r[:2], r[2:])]
    active, slope = gelu_parts(pre_act.astype(f32))
    act = active.astype(bf16)
    og_q[0], og_q[1], act = tie((og_q[0], og_q[1], act))
    with jax.named_scope("act_y"):
        b0, a0 = ring_first(act, "y")
    with jax.named_scope("og_swap"):
        three = jnp.stack([tok_q] + og_q).reshape(3, 4, 2, kt, kd)
        mine = jnp.where(first, three[:, :, 0], three[:, :, 1])
        theirs = jnp.where(first, three[:, :, 1], three[:, :, 0])
        theirs = shift(theirs, "core", 1, 2)
        three = jnp.concatenate([mine, theirs], -1)
    with jax.named_scope("og_zl"):
        got = [lax.dynamic_index_in_dim(three, (zl - r) % 4, 1, False) for r in range(4)]
        got = [got[0]] + [shift(got[r], "zl", -r) for r in range(1, 4)]
        got, b0, a0 = tie((got, b0, a0))
        tok, og = (jnp.concatenate([g[k, :, c : c + kd] for c in (0, kd) for g in got], 1) for k in (0, 1))
        swapped = [jnp.where(first, g[2], jnp.concatenate([g[2, :, kd:], g[2, :, :kd]], 1)) for g in got]
        og_h = jnp.concatenate(turned(swapped, -zl), 1)
    with jax.named_scope("act_y2"):
        act_all = jnp.concatenate(ring_second(act, b0, a0, "y"))
    with jax.named_scope("og_x"):
        flat = jnp.concatenate([og, og_h])
        b3, a3 = ring_first(flat, "x")
        b3, a3, act_all = tie((b3, a3, act_all))
        slots = ring_second(flat, b3, a3, "x")
        og = jnp.concatenate(turned([s[:kt] for s in slots], -x))
        og_h = jnp.concatenate(turned([s[kt:] for s in slots[:1] + slots[:0:-1]], x - y), 1)
    half = 4 * kd
    og, og_h = tie((og, og_h))

    def pre_grad_of(k):
        cols = slice(k * part, (k + 1) * part)
        return (jnp.dot(og_h, w_all[k], preferred_element_type=f32) * slope[:, cols]).astype(bf16)

    with jax.named_scope("hid_a"):
        pre_a = pre_grad_of(0)
        pre_a, tok, og = tie((pre_a, tok, og))
    with jax.named_scope("grad_y_a"):
        ba, aa = ring_first(pre_a, "y")
    with jax.named_scope("down"):
        blocks = product(og[:, :half], og[:, half:], act_all)
        ba, aa, blocks = tie((ba, aa, blocks))
        parts = spread(blocks)
    with jax.named_scope("tok_x"):
        b4, a4 = ring_first(tok, "x")
    with jax.named_scope("grad_y2_a"):
        grad_a = jnp.concatenate(ring_second(pre_a, ba, aa, "y"))
        grad_a, b4, a4, parts[0], parts[1] = tie((grad_a, b4, a4, parts[0], parts[1]))
    with jax.named_scope("tok_x2"):
        tok = jnp.concatenate(turned(ring_second(tok, b4, a4, "x"), -x))
    with jax.named_scope("hid_b"):
        pre_b = pre_grad_of(1)
    with jax.named_scope("grad_y_b"):
        bb, ab = ring_first(pre_b, "y")
    with jax.named_scope("up_a"):
        up_a = product(tok[:, :half], tok[:, half:], grad_a)
        bb, ab, up_a, parts[2] = tie((bb, ab, up_a, parts[2]))
        parts_a = spread(up_a)
    with jax.named_scope("grad_y2_b"):
        grad_b = jnp.concatenate(ring_second(pre_b, bb, ab, "y"))
        grad_b, parts_a[0], parts_a[1] = tie((grad_b, parts_a[0], parts_a[1]))
        down = total_of(blocks[0], parts)
    with jax.named_scope("up_b"):
        up_b = product(tok[:, :half], tok[:, half:], grad_b)
        up_b, parts_a[2] = tie((up_b, parts_a[2]))
        up_b = total_of(up_b[0], spread(up_b))
        up = jnp.concatenate([total_of(up_a[0], parts_a), up_b], 1)
    return (up, down)


def solution(mesh):
    fine = Mesh(mesh.devices.reshape(4, 4, 2, 2, 4), ROW + COL)
    return jax.shard_map(
        body,
        mesh=fine,
        in_specs=(P(None, ROW), P(COL, ROW), P(ROW, COL), P(ROW, COL)),
        out_specs=(P(ROW, COL), P(ROW, COL)),
        check_vma=False,
    )
```

```python
import math

import jax
import jax.numpy as jnp
from jax import lax
from jax.sharding import Mesh
from jax.sharding import PartitionSpec as P

ROW = ("y", "zl", "core")
COL = ("zh", "x")
bf16, f32 = jnp.bfloat16, jnp.float32
tie = lax.optimization_barrier


def gelu_parts(pre):
    scale_c = math.sqrt(2.0 / math.pi)
    inner = jnp.tanh(scale_c * (pre + 0.044715 * pre * pre * pre))
    active = 0.5 * pre * (1.0 + inner)
    slope = 0.5 * (1.0 + inner) + 0.5 * pre * (1.0 - inner * inner) * scale_c * (
        1.0 + 3.0 * 0.044715 * pre * pre
    )
    return (active, slope)


def shift(v, axis, by, size=4):
    return lax.ppermute(v, axis, [(i, (i + by) % size) for i in range(size)])


def ring_first(v, axis):
    return shift(v, axis, 1), shift(v, axis, -1)


def ring_second(v, before, after, axis):
    half = v.shape[0] // 2
    far = jnp.concatenate([shift(before[:half], axis, 1), shift(after[half:], axis, -1)])
    return [v, after, far, before]


def turned(slots, by):
    def pick(k):
        i = (k + by) % 4
        return jnp.where(i < 2, jnp.where(i == 0, slots[0], slots[1]), jnp.where(i == 2, slots[2], slots[3]))

    return [pick(k) for k in range(4)]


def dot_t(a, b):
    return lax.dot_general(a, b, (((0,), (0,)), ((), ())), preferred_element_type=f32)


def product(own, other, right):
    theirs = shift(dot_t(other, right), "core", 1, 2)
    mine, theirs = tie((dot_t(own, right), theirs))
    total = mine + theirs
    n = total.shape[0] // 4
    return [total[r * n : (r + 1) * n] for r in range(4)]


def spread(blocks):
    return [shift(blocks[r].astype(bf16), "zl", r) for r in (1, 3, 2)]


def total_of(own, others):
    for o in others:
        own = own + o.astype(f32)
    return own


def body(tokens_in, out_grad, pre_act, w_down):
    y, zl, core, zh, x = (lax.axis_index(a) for a in ("y", "zl", "core", "zh", "x"))
    first = core == 0
    kd, full = w_down.shape
    kt = pre_act.shape[0]
    w_all = lax.all_gather(w_down, ROW, axis=0, tiled=True)

    with jax.named_scope("quarter"):
        perms = ([], [], [], [])
        for yy in range(4):
            for hh in range(2):
                for xx in range(4):
                    dst = (yy * 2 + hh) * 4 + xx
                    for k in range(2):
                        qq = (xx + yy) % 4
                        perms[k].append(((yy * 2 + qq // 2) * 4 + 2 * (qq % 2) + (hh + k) % 2, dst))
                        src = ((yy - xx) % 4 * 2 + yy // 2) * 4 + 2 * (yy % 2) + (hh + k) % 2
                        perms[2 + k].append((src, dst))
        r = [lax.ppermute(out_grad, ("y", "zh", "x"), p) for p in perms]
        q = (x + y) % 4
        quarter = 2 * out_grad.shape[0]
        tok_q = lax.dynamic_slice_in_dim(tokens_in, q * quarter, quarter, 0)
        og_q = [jnp.concatenate([jnp.where(zh == 0, a, b), jnp.where(zh == 0, b, a)]) for a, b in (r[:2], r[2:])]
    active, slope = gelu_parts(pre_act.astype(f32))
    act = active.astype(bf16)
    og_q[0], og_q[1], act = tie((og_q[0], og_q[1], act))
    with jax.named_scope("act_y"):
        b0, a0 = ring_first(act, "y")
    with jax.named_scope("og_swap"):
        three = jnp.stack([tok_q] + og_q).reshape(3, 4, 2, kt, kd)
        mine = jnp.where(first, three[:, :, 0], three[:, :, 1])
        theirs = jnp.where(first, three[:, :, 1], three[:, :, 0])
        theirs = shift(theirs, "core", 1, 2)
        three = jnp.concatenate([mine, theirs], -1)
    with jax.named_scope("og_zl"):
        got = [lax.dynamic_index_in_dim(three, (zl - r) % 4, 1, False) for r in range(4)]
        got = [got[0]] + [shift(got[r], "zl", -r) for r in range(1, 4)]
        got, b0, a0 = tie((got, b0, a0))
        tok, og = (jnp.concatenate([g[k, :, c : c + kd] for c in (0, kd) for g in got], 1) for k in (0, 1))
        swapped = [jnp.where(first, g[2], jnp.concatenate([g[2, :, kd:], g[2, :, :kd]], 1)) for g in got]
        og_h = jnp.concatenate(turned(swapped, -zl), 1)
    with jax.named_scope("act_y2"):
        act_all = jnp.concatenate(ring_second(act, b0, a0, "y"))
    with jax.named_scope("og_x"):
        flat = jnp.concatenate([og, og_h])
        b3, a3 = ring_first(flat, "x")
        b3, a3, act_all = tie((b3, a3, act_all))
        slots = ring_second(flat, b3, a3, "x")
        slots = tie(slots)
        og = jnp.concatenate(turned([s[:kt] for s in slots], -x))
        og_h = jnp.concatenate(turned([s[kt:] for s in slots[:1] + slots[:0:-1]], x - y), 1)
    half = 4 * kd

    with jax.named_scope("down"):
        blocks = product(og[:, :half], og[:, half:], act_all)
        og_h, blocks, tok = tie((og_h, blocks, tok))
        parts = spread(blocks)
    with jax.named_scope("tok_x"):
        b4, a4 = ring_first(tok, "x")
    with jax.named_scope("hid"):
        hid = jnp.dot(og_h, w_all, preferred_element_type=f32)
        pre_grad = (hid * slope).astype(bf16)
    with jax.named_scope("grad_y"):
        pre_grad, parts[0] = tie((pre_grad, parts[0]))
        bb, aa = ring_first(pre_grad, "y")
        bb, aa, b4, a4 = tie((bb, aa, b4, a4))
    with jax.named_scope("tok_x2"):
        tok = jnp.concatenate(turned(ring_second(tok, b4, a4, "x"), -x))
    with jax.named_scope("grad_y2"):
        grad_all = jnp.concatenate(ring_second(pre_grad, bb, aa, "y"))
        grad_all, parts = tie((grad_all, parts))
    with jax.named_scope("up"):
        up = product(tok[:, :half], tok[:, half:], grad_all)
        down = total_of(blocks[0], parts)
        up = total_of(up[0], spread(up))
    return (up, down)


def solution(mesh):
    fine = Mesh(mesh.devices.reshape(4, 4, 2, 2, 4), ROW + COL)
    return jax.shard_map(
        body,
        mesh=fine,
        in_specs=(P(None, ROW), P(COL, ROW), P(ROW, COL), P(ROW, COL)),
        out_specs=(P(ROW, COL), P(ROW, COL)),
        check_vma=False,
    )
```

```python
import math

import jax
import jax.numpy as jnp
from jax import lax
from jax.sharding import Mesh
from jax.sharding import PartitionSpec as P

ROW = ("y", "zl", "core")
COL = ("zh", "x")
bf16, f32 = jnp.bfloat16, jnp.float32
tie = lax.optimization_barrier


def gelu_parts(pre):
    scale_c = math.sqrt(2.0 / math.pi)
    inner = jnp.tanh(scale_c * (pre + 0.044715 * pre * pre * pre))
    active = 0.5 * pre * (1.0 + inner)
    slope = 0.5 * (1.0 + inner) + 0.5 * pre * (1.0 - inner * inner) * scale_c * (
        1.0 + 3.0 * 0.044715 * pre * pre
    )
    return (active, slope)


def shift(v, axis, by, size=4):
    return lax.ppermute(v, axis, [(i, (i + by) % size) for i in range(size)])


def ring_first(v, axis):
    return shift(v, axis, 1), shift(v, axis, -1)


def ring_second(v, before, after, axis):
    half = v.shape[0] // 2
    far = jnp.concatenate([shift(before[:half], axis, 1), shift(after[half:], axis, -1)])
    return [v, after, far, before]


def turned(slots, by):
    def pick(k):
        i = (k + by) % 4
        return jnp.where(i < 2, jnp.where(i == 0, slots[0], slots[1]), jnp.where(i == 2, slots[2], slots[3]))

    return [pick(k) for k in range(4)]


def dot_t(a, b):
    return lax.dot_general(a, b, (((0,), (0,)), ((), ())), preferred_element_type=f32)


def product(own, other, right):
    theirs = shift(dot_t(other, right), "core", 1, 2)
    mine, theirs = tie((dot_t(own, right), theirs))
    total = mine + theirs
    n = total.shape[0] // 4
    return [total[r * n : (r + 1) * n] for r in range(4)]


def spread(blocks):
    return [shift(blocks[r].astype(bf16), "zl", r) for r in (1, 3, 2)]


def total_of(own, others):
    for o in others:
        own = own + o.astype(f32)
    return own


def body(tokens_in, out_grad, pre_act, w_down):
    y, zl, core, zh, x = (lax.axis_index(a) for a in ("y", "zl", "core", "zh", "x"))
    first = core == 0
    kd, full = w_down.shape
    kt = pre_act.shape[0]
    w_all = lax.all_gather(w_down, ROW, axis=0, tiled=True)

    with jax.named_scope("quarter"):
        perms = ([], [], [], [])
        for yy in range(4):
            for hh in range(2):
                for xx in range(4):
                    dst = (yy * 2 + hh) * 4 + xx
                    for k in range(2):
                        qq = (xx + yy) % 4
                        perms[k].append(((yy * 2 + qq // 2) * 4 + 2 * (qq % 2) + (hh + k) % 2, dst))
                        src = ((yy - xx) % 4 * 2 + yy // 2) * 4 + 2 * (yy % 2) + (hh + k) % 2
                        perms[2 + k].append((src, dst))
        r = [lax.ppermute(out_grad, ("y", "zh", "x"), p) for p in perms]
        q = (x + y) % 4
        quarter = 2 * out_grad.shape[0]
        tok_q = lax.dynamic_slice_in_dim(tokens_in, q * quarter, quarter, 0)
        og_q = [jnp.concatenate([jnp.where(zh == 0, a, b), jnp.where(zh == 0, b, a)]) for a, b in (r[:2], r[2:])]
    active, slope = gelu_parts(pre_act.astype(f32))
    act = active.astype(bf16)
    og_q[0], og_q[1], act = tie((og_q[0], og_q[1], act))
    with jax.named_scope("act_y"):
        b0, a0 = ring_first(act, "y")
    with jax.named_scope("og_swap"):
        three = jnp.stack([tok_q] + og_q).reshape(3, 4, 2, kt, kd)
        mine = jnp.where(first, three[:, :, 0], three[:, :, 1])
        theirs = jnp.where(first, three[:, :, 1], three[:, :, 0])
        theirs = shift(theirs, "core", 1, 2)
        three = jnp.concatenate([mine, theirs], -1)
    with jax.named_scope("og_zl"):
        got = [lax.dynamic_index_in_dim(three, (zl - r) % 4, 1, False) for r in range(4)]
        got = [got[0]] + [shift(got[r], "zl", -r) for r in range(1, 4)]
        got, b0, a0 = tie((got, b0, a0))
        tok = jnp.concatenate([g[0, :, c : c + kd] for c in (0, kd) for g in got], 1)
        og = turned([g[1] for g in got], -zl)
        og = jnp.concatenate([g[:, c : c + kd] for c in (0, kd) for g in og], 1)
        swapped = [jnp.where(first, g[2], jnp.concatenate([g[2, :, kd:], g[2, :, :kd]], 1)) for g in got]
        og_h = jnp.concatenate(turned(swapped, -zl), 1)
    with jax.named_scope("act_y2"):
        act_all = jnp.concatenate(ring_second(act, b0, a0, "y"))
    with jax.named_scope("og_x"):
        flat = jnp.concatenate([og, og_h])
        b3, a3 = ring_first(flat, "x")
        b3, a3, act_all = tie((b3, a3, act_all))
        slots = ring_second(flat, b3, a3, "x")
        slots = tie(slots)
        og = jnp.concatenate(turned([s[:kt] for s in slots], -x))
        og_h = jnp.concatenate(turned([s[kt:] for s in slots[:1] + slots[:0:-1]], x - y), 1)
    half = 4 * kd

    with jax.named_scope("down"):
        theirs = dot_t(og[:, half:], act_all)
        theirs, tok, og = tie((theirs, tok, og))
        theirs = shift(theirs, "core", 1, 2)
    with jax.named_scope("tok_x"):
        b4, a4 = ring_first(tok, "x")
    with jax.named_scope("down"):
        mine, theirs = tie((dot_t(og[:, :half], act_all), theirs))
        total = (mine + theirs).reshape(4, kd, full)
        down_own = lax.dynamic_index_in_dim(total, zl, 0, False)
        place = lax.broadcasted_iota(jnp.int32, total.shape, 0)
        total = jnp.where(place == zl, 0.0, total).astype(bf16).reshape(4 * kd, full)
        og_h, total = tie((og_h, total))
        summed = lax.psum_scatter(total, "zl", scatter_dimension=0, tiled=True)
    with jax.named_scope("hid"):
        hid = jnp.dot(og_h, w_all, preferred_element_type=f32)
        pre_grad = (hid * slope).astype(bf16)
    with jax.named_scope("grad_y"):
        pre_grad, b4, a4 = tie((pre_grad, b4, a4))
        bb, aa = ring_first(pre_grad, "y")
        bb, aa, b4, a4 = tie((bb, aa, b4, a4))
    with jax.named_scope("tok_x2"):
        tok = jnp.concatenate(turned(ring_second(tok, b4, a4, "x"), -x))
    with jax.named_scope("grad_y2"):
        grad_all = jnp.concatenate(ring_second(pre_grad, bb, aa, "y"))
    with jax.named_scope("up"):
        grad_all, summed = tie((grad_all, summed))
        down = down_own + summed.astype(f32)
        up = product(tok[:, :half], tok[:, half:], grad_all)
        up = total_of(up[0], spread(up))
    return (up, down)


def solution(mesh):
    fine = Mesh(mesh.devices.reshape(4, 4, 2, 2, 4), ROW + COL)
    return jax.shard_map(
        body,
        mesh=fine,
        in_specs=(P(None, ROW), P(COL, ROW), P(ROW, COL), P(ROW, COL)),
        out_specs=(P(ROW, COL), P(ROW, COL)),
        check_vma=False,
    )
```

```python
import math

import jax
import jax.numpy as jnp
from jax import lax
from jax.sharding import Mesh
from jax.sharding import PartitionSpec as P

ROW = ("y", "zl", "core")
COL = ("zh", "x")
bf16, f32 = jnp.bfloat16, jnp.float32
tie = lax.optimization_barrier


def gelu_parts(pre):
    scale_c = math.sqrt(2.0 / math.pi)
    inner = jnp.tanh(scale_c * (pre + 0.044715 * pre * pre * pre))
    active = 0.5 * pre * (1.0 + inner)
    slope = 0.5 * (1.0 + inner) + 0.5 * pre * (1.0 - inner * inner) * scale_c * (
        1.0 + 3.0 * 0.044715 * pre * pre
    )
    return (active, slope)


def shift(v, axis, by, size=4):
    return lax.ppermute(v, axis, [(i, (i + by) % size) for i in range(size)])


def ring_first(v, axis):
    return shift(v, axis, 1), shift(v, axis, -1)


def ring_second(v, before, after, axis):
    half = v.shape[0] // 2
    far = jnp.concatenate([shift(before[:half], axis, 1), shift(after[half:], axis, -1)])
    return [v, after, far, before]


def turned(slots, by):
    def pick(k):
        i = (k + by) % 4
        return jnp.where(i < 2, jnp.where(i == 0, slots[0], slots[1]), jnp.where(i == 2, slots[2], slots[3]))

    return [pick(k) for k in range(4)]


def dot_t(a, b):
    return lax.dot_general(a, b, (((0,), (0,)), ((), ())), preferred_element_type=f32)


def product(own, other, right):
    theirs = shift(dot_t(other, right), "core", 1, 2)
    mine, theirs = tie((dot_t(own, right), theirs))
    total = mine + theirs
    n = total.shape[0] // 4
    return [total[r * n : (r + 1) * n] for r in range(4)]


def spread(blocks):
    return [shift(blocks[r].astype(bf16), "zl", r) for r in (1, 3, 2)]


def total_of(own, others):
    for o in others:
        own = own + o.astype(f32)
    return own


def body(tokens_in, out_grad, pre_act, w_down):
    y, zl, core, zh, x = (lax.axis_index(a) for a in ("y", "zl", "core", "zh", "x"))
    first = core == 0
    kd, full = w_down.shape
    kt = pre_act.shape[0]
    w_all = lax.all_gather(w_down, ROW, axis=0, tiled=True)

    with jax.named_scope("pre_y"):
        b0, a0 = ring_first(pre_act, "y")
    with jax.named_scope("quarter"):
        perms = ([], [])
        for yy in range(4):
            for hh in range(2):
                for xx in range(4):
                    for k in range(2):
                        qq = (xx + yy) % 4
                        src = (yy * 2 + qq // 2) * 4 + 2 * (qq % 2) + (hh + k) % 2
                        perms[k].append((src, (yy * 2 + hh) * 4 + xx))
        r0, r1 = (lax.ppermute(out_grad, ("y", "zh", "x"), p) for p in perms)
        quarter = 2 * out_grad.shape[0]
        tok = lax.dynamic_slice_in_dim(tokens_in, (x + y) % 4 * quarter, quarter, 0)
        og = jnp.concatenate([jnp.where(zh == 0, r0, r1), jnp.where(zh == 0, r1, r0)])
    with jax.named_scope("core"):
        two = jnp.stack([tok, og]).reshape(2, 4, 2, kt, kd)
        mine = jnp.where(first, two[:, :, 0], two[:, :, 1])
        theirs = jnp.where(first, two[:, :, 1], two[:, :, 0])
        two = jnp.concatenate([mine, shift(theirs, "core", 1, 2)], -1)
    with jax.named_scope("zl"):
        got = [lax.dynamic_index_in_dim(two, (zl - r) % 4, 1, False) for r in range(4)]
        got = [got[0]] + [shift(got[r], "zl", -r) for r in range(1, 4)]
        got, b0, a0 = tie((got, b0, a0))
        tok, og = (jnp.concatenate([g[k, :, c : c + kd] for c in (0, kd) for g in got], 1) for k in (0, 1))
    with jax.named_scope("og_x"):
        b3, a3 = ring_first(og, "x")
    with jax.named_scope("pre_y2"):
        pre_all = jnp.concatenate(turned(ring_second(pre_act, b0, a0, "y"), -y))
        b3, a3, pre_all = tie((b3, a3, pre_all))
        active, slope = gelu_parts(pre_all.astype(f32))
        act_all = active.astype(bf16)
    half = 4 * kd
    with jax.named_scope("og_x2"):
        slots = tie(ring_second(og, b3, a3, "x"))
        og = jnp.concatenate(turned(slots, -x - y))
    with jax.named_scope("og_y"):
        pieces = [(og[:, r * kd : (r + 1) * kd], og[:, half + r * kd : half + (r + 1) * kd]) for r in range(4)]
        pieces = [jnp.where(first, jnp.concatenate([u, v], 1), jnp.concatenate([v, u], 1)) for u, v in pieces]
        og_h = jnp.concatenate(turned(pieces, -zl), 1)
        b5, a5 = ring_first(og_h, "y")
    with jax.named_scope("down"):
        blocks = product(og[:, :half], og[:, half:], act_all)
        b5, a5, blocks, tok = tie((b5, a5, blocks, tok))
        parts = spread(blocks)
    with jax.named_scope("tok_x"):
        b4, a4 = ring_first(tok, "x")
    with jax.named_scope("og_y2"):
        slots = ring_second(og_h, b5, a5, "y")
        slots, parts[0], parts[1], b4, a4 = tie((slots, parts[0], parts[1], b4, a4))
    with jax.named_scope("tok_x2"):
        tok = jnp.concatenate(turned(ring_second(tok, b4, a4, "x"), -x - y))
    with jax.named_scope("hid"):
        hid = None
        for r in range(4):
            w_r = lax.dynamic_slice_in_dim(w_all, (y + r) % 4 * 2 * half, 2 * half, 0)
            term = jnp.dot(slots[r], w_r, preferred_element_type=f32)
            hid = term if hid is None else hid + term
        pre_grad = (hid * slope).astype(bf16)
        pre_grad, parts[2], tok = tie((pre_grad, parts[2], tok))
    with jax.named_scope("up"):
        up = product(tok[:, :half], tok[:, half:], pre_grad)
        down = total_of(blocks[0], parts)
        up = total_of(up[0], spread(up))
    return (up, down)


def solution(mesh):
    fine = Mesh(mesh.devices.reshape(4, 4, 2, 2, 4), ROW + COL)
    return jax.shard_map(
        body,
        mesh=fine,
        in_specs=(P(None, ROW), P(COL, ROW), P(ROW, COL), P(ROW, COL)),
        out_specs=(P(ROW, COL), P(ROW, COL)),
        check_vma=False,
    )
```

```python
import math

import jax
import jax.numpy as jnp
from jax import lax
from jax.sharding import Mesh
from jax.sharding import PartitionSpec as P

ROW = ("y", "zl", "core")
COL = ("zh", "x")
bf16, f32 = jnp.bfloat16, jnp.float32
tie = lax.optimization_barrier


def gelu_parts(pre):
    scale_c = math.sqrt(2.0 / math.pi)
    inner = jnp.tanh(scale_c * (pre + 0.044715 * pre * pre * pre))
    active = 0.5 * pre * (1.0 + inner)
    slope = 0.5 * (1.0 + inner) + 0.5 * pre * (1.0 - inner * inner) * scale_c * (
        1.0 + 3.0 * 0.044715 * pre * pre
    )
    return (active, slope)


def shift(v, axis, by, size=4):
    return lax.ppermute(v, axis, [(i, (i + by) % size) for i in range(size)])


def ring_first(v, axis):
    return shift(v, axis, 1), shift(v, axis, -1)


def ring_second(v, before, after, axis):
    half = v.shape[0] // 2
    far = jnp.concatenate([shift(before[:half], axis, 1), shift(after[half:], axis, -1)])
    return [v, after, far, before]


def turned(slots, by):
    def pick(k):
        i = (k + by) % 4
        return jnp.where(i < 2, jnp.where(i == 0, slots[0], slots[1]), jnp.where(i == 2, slots[2], slots[3]))

    return [pick(k) for k in range(4)]


def dot_t(a, b):
    return lax.dot_general(a, b, (((0,), (0,)), ((), ())), preferred_element_type=f32)


def product(own, other, right):
    theirs = shift(dot_t(other, right), "core", 1, 2)
    mine, theirs = tie((dot_t(own, right), theirs))
    total = mine + theirs
    n = total.shape[0] // 4
    return [total[r * n : (r + 1) * n] for r in range(4)]


def spread(blocks):
    return [shift(blocks[r].astype(bf16), "zl", r) for r in (1, 3, 2)]


def total_of(own, others):
    for o in others:
        own = own + o.astype(f32)
    return own


def body(tokens_in, out_grad, pre_act, w_down):
    y, zl, core, zh, x = (lax.axis_index(a) for a in ("y", "zl", "core", "zh", "x"))
    first = core == 0
    kd, full = w_down.shape
    kt = pre_act.shape[0]
    w_all = lax.all_gather(w_down, ROW, axis=0, tiled=True)

    with jax.named_scope("pre_y"):
        b0, a0 = ring_first(pre_act, "y")
    with jax.named_scope("quarter"):
        perms = ([], [])
        for yy in range(4):
            for hh in range(2):
                for xx in range(4):
                    for k in range(2):
                        qq = (xx + yy) % 4
                        src = (yy * 2 + qq // 2) * 4 + 2 * (qq % 2) + (hh + k) % 2
                        perms[k].append((src, (yy * 2 + hh) * 4 + xx))
        r0, r1 = (lax.ppermute(out_grad, ("y", "zh", "x"), p) for p in perms)
        quarter = 2 * out_grad.shape[0]
        tok = lax.dynamic_slice_in_dim(tokens_in, (x + y) % 4 * quarter, quarter, 0)
        og = jnp.concatenate([jnp.where(zh == 0, r0, r1), jnp.where(zh == 0, r1, r0)])
    with jax.named_scope("core"):
        two = jnp.stack([tok, og]).reshape(2, 4, 2, kt, kd)
        mine = jnp.where(first, two[:, :, 0], two[:, :, 1])
        theirs = jnp.where(first, two[:, :, 1], two[:, :, 0])
        two = jnp.concatenate([mine, shift(theirs, "core", 1, 2)], -1)
    with jax.named_scope("zl"):
        got = [lax.dynamic_index_in_dim(two, (zl - r) % 4, 1, False) for r in range(4)]
        got = [got[0]] + [shift(got[r], "zl", -r) for r in range(1, 4)]
        got, b0, a0 = tie((got, b0, a0))
        tok, og = (jnp.concatenate([g[k, :, c : c + kd] for c in (0, kd) for g in got], 1) for k in (0, 1))
    with jax.named_scope("og_x"):
        b3, a3 = ring_first(og, "x")
    with jax.named_scope("pre_y2"):
        pre_all = jnp.concatenate(turned(ring_second(pre_act, b0, a0, "y"), -y))
        b3, a3, pre_all = tie((b3, a3, pre_all))
        active, slope = gelu_parts(pre_all.astype(f32))
        act_all = active.astype(bf16)
    half = 4 * kd
    with jax.named_scope("og_x2"):
        slots = tie(ring_second(og, b3, a3, "x"))
        og = jnp.concatenate(turned(slots, -x - y))
    with jax.named_scope("og_y"):
        pieces = [(og[:, r * kd : (r + 1) * kd], og[:, half + r * kd : half + (r + 1) * kd]) for r in range(4)]
        pieces = [jnp.where(first, jnp.concatenate([u, v], 1), jnp.concatenate([v, u], 1)) for u, v in pieces]
        og_h = jnp.concatenate(turned(pieces, -zl), 1)
        b5, a5 = ring_first(og_h, "y")
    with jax.named_scope("down"):
        blocks = product(og[:, :half], og[:, half:], act_all)
        blocks, tok = tie((blocks, tok))
        parts = spread(blocks)
    with jax.named_scope("tok_x"):
        b4, a4 = ring_first(tok, "x")
        toks = ring_second(tok, b4, a4, "x")
        b5, a5, parts[0], parts[1], toks = tie((b5, a5, parts[0], parts[1], toks))

    def term(v, r):
        w_r = lax.dynamic_slice_in_dim(w_all, (y + r) % 4 * 2 * half, 2 * half, 0)
        return jnp.dot(v, w_r, preferred_element_type=f32)

    with jax.named_scope("og_y2"):
        near = b5.shape[0] // 2
        far = [shift(b5[:near], "y", 1), shift(a5[near:], "y", -1)]
    with jax.named_scope("hid"):
        hid = term(og_h, 0) + term(a5, 1) + term(b5, 3)
        hid, far, parts[2] = tie((hid, far, parts[2]))
        hid = hid + term(jnp.concatenate(far), 2)
        pre_grad = (hid * slope).astype(bf16)
    with jax.named_scope("up"):
        tok = jnp.concatenate(turned(toks, -x - y))
        up = product(tok[:, :half], tok[:, half:], pre_grad)
        down = total_of(blocks[0], parts)
        up = total_of(up[0], spread(up))
    return (up, down)


def solution(mesh):
    fine = Mesh(mesh.devices.reshape(4, 4, 2, 2, 4), ROW + COL)
    return jax.shard_map(
        body,
        mesh=fine,
        in_specs=(P(None, ROW), P(COL, ROW), P(ROW, COL), P(ROW, COL)),
        out_specs=(P(ROW, COL), P(ROW, COL)),
        check_vma=False,
    )
```

```python
import math

import jax
import jax.numpy as jnp
from jax import lax
from jax.sharding import Mesh
from jax.sharding import PartitionSpec as P

ROW = ("y", "zl", "core")
COL = ("zh", "x")
bf16, f32 = jnp.bfloat16, jnp.float32
tie = lax.optimization_barrier


def gelu_parts(pre):
    scale_c = math.sqrt(2.0 / math.pi)
    inner = jnp.tanh(scale_c * (pre + 0.044715 * pre * pre * pre))
    active = 0.5 * pre * (1.0 + inner)
    slope = 0.5 * (1.0 + inner) + 0.5 * pre * (1.0 - inner * inner) * scale_c * (
        1.0 + 3.0 * 0.044715 * pre * pre
    )
    return (active, slope)


def shift(v, axis, by, size=4):
    return lax.ppermute(v, axis, [(i, (i + by) % size) for i in range(size)])


def ring_first(v, axis):
    return shift(v, axis, 1), shift(v, axis, -1)


def ring_second(v, before, after, axis):
    half = v.shape[0] // 2
    far = jnp.concatenate([shift(before[:half], axis, 1), shift(after[half:], axis, -1)])
    return [v, after, far, before]


def turned(slots, by):
    def pick(k):
        i = (k + by) % 4
        return jnp.where(i < 2, jnp.where(i == 0, slots[0], slots[1]), jnp.where(i == 2, slots[2], slots[3]))

    return [pick(k) for k in range(4)]


def dot_t(a, b):
    return lax.dot_general(a, b, (((0,), (0,)), ((), ())), preferred_element_type=f32)


def product(own, other, right, sent=f32):
    theirs = shift(dot_t(other, right).astype(sent), "core", 1, 2)
    mine, theirs = tie((dot_t(own, right), theirs))
    total = mine + theirs.astype(f32)
    n = total.shape[0] // 4
    return [total[r * n : (r + 1) * n] for r in range(4)]


def spread(blocks):
    return [shift(blocks[r].astype(bf16), "zl", r) for r in (1, 3, 2)]


def total_of(own, others):
    for o in others:
        own = own + o.astype(f32)
    return own


def body(tokens_in, out_grad, pre_act, w_down):
    y, zl, core, zh, x = (lax.axis_index(a) for a in ("y", "zl", "core", "zh", "x"))
    first = core == 0
    kd, full = w_down.shape
    kt = pre_act.shape[0]
    w_all = lax.all_gather(w_down, ROW, axis=0, tiled=True)

    with jax.named_scope("pre_y"):
        b0, a0 = ring_first(pre_act, "y")
    with jax.named_scope("quarter"):
        perms = ([], [])
        for yy in range(4):
            for hh in range(2):
                for xx in range(4):
                    for k in range(2):
                        qq = (xx + yy) % 4
                        src = (yy * 2 + qq // 2) * 4 + 2 * (qq % 2) + (hh + k) % 2
                        perms[k].append((src, (yy * 2 + hh) * 4 + xx))
        r0, r1 = (lax.ppermute(out_grad, ("y", "zh", "x"), p) for p in perms)
        quarter = 2 * out_grad.shape[0]
        tok = lax.dynamic_slice_in_dim(tokens_in, (x + y) % 4 * quarter, quarter, 0)
        og = jnp.concatenate([jnp.where(zh == 0, r0, r1), jnp.where(zh == 0, r1, r0)])
    with jax.named_scope("core"):
        two = jnp.stack([tok, og]).reshape(2, 4, 2, kt, kd)
        mine = jnp.where(first, two[:, :, 0], two[:, :, 1])
        theirs = jnp.where(first, two[:, :, 1], two[:, :, 0])
        two = jnp.concatenate([mine, shift(theirs, "core", 1, 2)], -1)
    with jax.named_scope("zl"):
        got = [lax.dynamic_index_in_dim(two, (zl - r) % 4, 1, False) for r in range(4)]
        got = [got[0]] + [shift(got[r], "zl", -r) for r in range(1, 4)]
        got, b0, a0 = tie((got, b0, a0))
        tok, og = (jnp.concatenate([g[k, :, c : c + kd] for c in (0, kd) for g in got], 1) for k in (0, 1))
    with jax.named_scope("og_x"):
        b3, a3 = ring_first(og, "x")
    with jax.named_scope("pre_y2"):
        pre_all = jnp.concatenate(turned(ring_second(pre_act, b0, a0, "y"), -y))
        b3, a3, pre_all = tie((b3, a3, pre_all))
        active, slope = gelu_parts(pre_all.astype(f32))
        act_all = active.astype(bf16)
    half = 4 * kd
    with jax.named_scope("og_x2"):
        slots = tie(ring_second(og, b3, a3, "x"))
        og = jnp.concatenate(turned(slots, -x - y))
    with jax.named_scope("og_y"):
        pieces = [(og[:, r * kd : (r + 1) * kd], og[:, half + r * kd : half + (r + 1) * kd]) for r in range(4)]
        pieces = [jnp.where(first, jnp.concatenate([u, v], 1), jnp.concatenate([v, u], 1)) for u, v in pieces]
        og_h = jnp.concatenate(turned(pieces, -zl), 1)
        b5, a5 = ring_first(og_h, "y")
    with jax.named_scope("down"):
        blocks = product(og[:, :half], og[:, half:], act_all)
        blocks, tok = tie((blocks, tok))
        parts = spread(blocks)
    with jax.named_scope("tok_x"):
        b4, a4 = ring_first(tok, "x")
        b5, a5, parts[0], b4, a4 = tie((b5, a5, parts[0], b4, a4))

    def term(v, r):
        w_r = lax.dynamic_slice_in_dim(w_all, (y + r) % 4 * 2 * half, 2 * half, 0)
        return jnp.dot(v, w_r, preferred_element_type=f32)

    with jax.named_scope("og_y2"):
        near = b5.shape[0] // 2
        far = [shift(b5[:near], "y", 1), shift(a5[near:], "y", -1)]
    with jax.named_scope("tok_x2"):
        toks = ring_second(tok, b4, a4, "x")
    with jax.named_scope("hid"):
        hid = term(og_h, 0) + term(a5, 1) + term(b5, 3)
        hid, far, parts[1], parts[2], toks = tie((hid, far, parts[1], parts[2], toks))
        hid = hid + term(jnp.concatenate(far), 2)
        pre_grad = (hid * slope).astype(bf16)
    with jax.named_scope("up"):
        tok = jnp.concatenate(turned(toks, -x - y))
        up = product(tok[:, :half], tok[:, half:], pre_grad, bf16)
        down = total_of(blocks[0], parts)
        up = total_of(up[0], spread(up))
    return (up, down)


def solution(mesh):
    fine = Mesh(mesh.devices.reshape(4, 4, 2, 2, 4), ROW + COL)
    return jax.shard_map(
        body,
        mesh=fine,
        in_specs=(P(None, ROW), P(COL, ROW), P(ROW, COL), P(ROW, COL)),
        out_specs=(P(ROW, COL), P(ROW, COL)),
        check_vma=False,
    )
```

```python
import math

import jax
import jax.numpy as jnp
from jax import lax
from jax.sharding import Mesh
from jax.sharding import PartitionSpec as P

ROW = ("y", "zl", "core")
COL = ("zh", "x")
bf16, f32 = jnp.bfloat16, jnp.float32
tie = lax.optimization_barrier


def gelu_parts(pre):
    scale_c = math.sqrt(2.0 / math.pi)
    inner = jnp.tanh(scale_c * (pre + 0.044715 * pre * pre * pre))
    active = 0.5 * pre * (1.0 + inner)
    slope = 0.5 * (1.0 + inner) + 0.5 * pre * (1.0 - inner * inner) * scale_c * (
        1.0 + 3.0 * 0.044715 * pre * pre
    )
    return (active, slope)


def shift(v, axis, by, size=4):
    return lax.ppermute(v, axis, [(i, (i + by) % size) for i in range(size)])


def ring_first(v, axis):
    return shift(v, axis, 1), shift(v, axis, -1)


def ring_second(v, before, after, axis):
    half = v.shape[0] // 2
    far = jnp.concatenate([shift(before[:half], axis, 1), shift(after[half:], axis, -1)])
    return [v, after, far, before]


def turned(slots, by):
    def pick(k):
        i = (k + by) % 4
        return jnp.where(i < 2, jnp.where(i == 0, slots[0], slots[1]), jnp.where(i == 2, slots[2], slots[3]))

    return [pick(k) for k in range(4)]


def dot_t(a, b):
    return lax.dot_general(a, b, (((0,), (0,)), ((), ())), preferred_element_type=f32)


def product(own, other, right, sent=f32):
    theirs = shift(dot_t(other, right).astype(sent), "core", 1, 2)
    mine, theirs = tie((dot_t(own, right), theirs))
    total = mine + theirs.astype(f32)
    n = total.shape[0] // 4
    return [total[r * n : (r + 1) * n] for r in range(4)]


def spread(blocks):
    return [shift(blocks[r].astype(bf16), "zl", r) for r in (1, 3, 2)]


def total_of(own, others):
    for o in others:
        own = own + o.astype(f32)
    return own


def body(tokens_in, out_grad, pre_act, w_down):
    y, zl, core, zh, x = (lax.axis_index(a) for a in ("y", "zl", "core", "zh", "x"))
    first = core == 0
    kd, full = w_down.shape
    kt = pre_act.shape[0]
    w_all = lax.all_gather(w_down, ROW, axis=0, tiled=True)

    with jax.named_scope("pre_y"):
        b0, a0 = ring_first(pre_act, "y")
    with jax.named_scope("quarter"):
        perms = ([], [])
        for yy in range(4):
            for hh in range(2):
                for xx in range(4):
                    for k in range(2):
                        qq = (xx + yy) % 4
                        src = (yy * 2 + qq // 2) * 4 + 2 * (qq % 2) + (hh + k) % 2
                        perms[k].append((src, (yy * 2 + hh) * 4 + xx))
        r0, r1 = (lax.ppermute(out_grad, ("y", "zh", "x"), p) for p in perms)
        quarter = 2 * out_grad.shape[0]
        tok = lax.dynamic_slice_in_dim(tokens_in, (x + y) % 4 * quarter, quarter, 0)
        og = jnp.concatenate([jnp.where(zh == 0, r0, r1), jnp.where(zh == 0, r1, r0)])
    with jax.named_scope("core"):
        two = jnp.stack([tok, og]).reshape(2, 4, 2, kt, kd)
        mine = jnp.where(first, two[:, :, 0], two[:, :, 1])
        theirs = jnp.where(first, two[:, :, 1], two[:, :, 0])
        two = jnp.concatenate([mine, shift(theirs, "core", 1, 2)], -1)
    with jax.named_scope("zl"):
        got = [lax.dynamic_index_in_dim(two, (zl - r) % 4, 1, False) for r in range(4)]
        got = [got[0]] + [shift(got[r], "zl", -r) for r in range(1, 4)]
        got, b0, a0 = tie((got, b0, a0))
        tok, og = (jnp.concatenate([g[k, :, c : c + kd] for c in (0, kd) for g in got], 1) for k in (0, 1))
    with jax.named_scope("og_x"):
        b3, a3 = ring_first(og, "x")
    with jax.named_scope("pre_y2"):
        pre_all = jnp.concatenate(turned(ring_second(pre_act, b0, a0, "y"), -y))
        b3, a3, pre_all = tie((b3, a3, pre_all))
        active, slope = gelu_parts(pre_all.astype(f32))
        act_all = active.astype(bf16)
    half = 4 * kd
    with jax.named_scope("og_x2"):
        slots = tie(ring_second(og, b3, a3, "x"))
        og = jnp.concatenate(turned(slots, -x - y))
    with jax.named_scope("og_y"):
        pieces = [(og[:, r * kd : (r + 1) * kd], og[:, half + r * kd : half + (r + 1) * kd]) for r in range(4)]
        pieces = [jnp.where(first, jnp.concatenate([u, v], 1), jnp.concatenate([v, u], 1)) for u, v in pieces]
        og_h = jnp.concatenate(turned(pieces, -zl), 1)
        b5, a5 = ring_first(og_h, "y")
    with jax.named_scope("down"):
        blocks = product(og[:, :half], og[:, half:], act_all)
        blocks, tok = tie((blocks, tok))
        parts = [shift(blocks[1].astype(bf16), "zl", 1)]
    with jax.named_scope("tok_x"):
        b4, a4 = ring_first(tok, "x")
        b5, a5, parts[0], b4, a4 = tie((b5, a5, parts[0], b4, a4))

    def term(v, r):
        w_r = lax.dynamic_slice_in_dim(w_all, (y + r) % 4 * 2 * half, 2 * half, 0)
        return jnp.dot(v, w_r, preferred_element_type=f32)

    with jax.named_scope("og_y2"):
        near = b5.shape[0] // 2
        far = [shift(b5[:near], "y", 1), shift(a5[near:], "y", -1)]
    with jax.named_scope("hid"):
        hid = term(og_h, 0)
        hid, b4, a4, blocks[2], blocks[3] = tie((hid, b4, a4, blocks[2], blocks[3]))
    with jax.named_scope("down"):
        parts += [shift(blocks[r].astype(bf16), "zl", r) for r in (3, 2)]
    with jax.named_scope("tok_x2"):
        toks = ring_second(tok, b4, a4, "x")
    with jax.named_scope("hid"):
        hid = hid + term(a5, 1) + term(b5, 3)
        hid, far, parts[1], toks = tie((hid, far, parts[1], toks))
        hid = hid + term(jnp.concatenate(far), 2)
        pre_grad = (hid * slope).astype(bf16)
    with jax.named_scope("up"):
        tok = jnp.concatenate(turned(toks, -x - y))
        pre_grad, parts[2] = tie((pre_grad, parts[2]))
        up = product(tok[:, :half], tok[:, half:], pre_grad, bf16)
        down = total_of(blocks[0], parts)
        up = total_of(up[0], spread(up))
    return (up, down)


def solution(mesh):
    fine = Mesh(mesh.devices.reshape(4, 4, 2, 2, 4), ROW + COL)
    return jax.shard_map(
        body,
        mesh=fine,
        in_specs=(P(None, ROW), P(COL, ROW), P(ROW, COL), P(ROW, COL)),
        out_specs=(P(ROW, COL), P(ROW, COL)),
        check_vma=False,
    )
```

```python
import math

import jax
import jax.numpy as jnp
from jax import lax
from jax.sharding import Mesh
from jax.sharding import PartitionSpec as P

ROW = ("y", "zl", "core")
COL = ("zh", "x")
bf16, f32 = jnp.bfloat16, jnp.float32
tie = lax.optimization_barrier


def gelu_parts(pre):
    scale_c = math.sqrt(2.0 / math.pi)
    inner = jnp.tanh(scale_c * (pre + 0.044715 * pre * pre * pre))
    active = 0.5 * pre * (1.0 + inner)
    slope = 0.5 * (1.0 + inner) + 0.5 * pre * (1.0 - inner * inner) * scale_c * (
        1.0 + 3.0 * 0.044715 * pre * pre
    )
    return (active, slope)


def shift(v, axis, by, size=4):
    return lax.ppermute(v, axis, [(i, (i + by) % size) for i in range(size)])


def ring_first(v, axis):
    return shift(v, axis, 1), shift(v, axis, -1)


def ring_second(v, before, after, axis):
    half = v.shape[0] // 2
    far = jnp.concatenate([shift(before[:half], axis, 1), shift(after[half:], axis, -1)])
    return [v, after, far, before]


def turned(slots, by):
    def pick(k):
        i = (k + by) % 4
        return jnp.where(i < 2, jnp.where(i == 0, slots[0], slots[1]), jnp.where(i == 2, slots[2], slots[3]))

    return [pick(k) for k in range(4)]


def dot_t(a, b):
    return lax.dot_general(a, b, (((0,), (0,)), ((), ())), preferred_element_type=f32)


def product(own, other, right, sent=f32):
    theirs = shift(dot_t(other, right).astype(sent), "core", 1, 2)
    mine, theirs = tie((dot_t(own, right), theirs))
    total = mine + theirs.astype(f32)
    n = total.shape[0] // 4
    return [total[r * n : (r + 1) * n] for r in range(4)]


def spread(blocks):
    return [shift(blocks[r].astype(bf16), "zl", r) for r in (1, 3, 2)]


def total_of(own, others):
    for o in others:
        own = own + o.astype(f32)
    return own


def body(tokens_in, out_grad, pre_act, w_down):
    y, zl, core, zh, x = (lax.axis_index(a) for a in ("y", "zl", "core", "zh", "x"))
    first = core == 0
    kd, full = w_down.shape
    kt = pre_act.shape[0]
    w_all = lax.all_gather(w_down, ROW, axis=0, tiled=True)

    with jax.named_scope("pre_y"):
        b0, a0 = ring_first(pre_act, "y")
    with jax.named_scope("quarter"):
        perms = ([], [])
        for yy in range(4):
            for hh in range(2):
                for xx in range(4):
                    for k in range(2):
                        qq = (xx + yy) % 4
                        src = (yy * 2 + qq // 2) * 4 + 2 * (qq % 2) + (hh + k) % 2
                        perms[k].append((src, (yy * 2 + hh) * 4 + xx))
        r0, r1 = (lax.ppermute(out_grad, ("y", "zh", "x"), p) for p in perms)
        quarter = 2 * out_grad.shape[0]
        tok = lax.dynamic_slice_in_dim(tokens_in, (x + y) % 4 * quarter, quarter, 0)
        og = jnp.concatenate([jnp.where(zh == 0, r0, r1), jnp.where(zh == 0, r1, r0)])
    with jax.named_scope("core"):
        two = jnp.stack([tok, og]).reshape(2, 4, 2, kt, kd)
        mine = jnp.where(first, two[:, :, 0], two[:, :, 1])
        theirs = jnp.where(first, two[:, :, 1], two[:, :, 0])
        two = jnp.concatenate([mine, shift(theirs, "core", 1, 2)], -1)
    with jax.named_scope("zl"):
        got = [lax.dynamic_index_in_dim(two, (zl - r) % 4, 1, False) for r in range(4)]
        got = [got[0]] + [shift(got[r], "zl", -r) for r in range(1, 4)]
        got, b0, a0 = tie((got, b0, a0))
        tok, og = (jnp.concatenate([g[k, :, c : c + kd] for c in (0, kd) for g in got], 1) for k in (0, 1))
    with jax.named_scope("og_x"):
        b3, a3 = ring_first(og, "x")
    with jax.named_scope("pre_y2"):
        pre_all = jnp.concatenate(turned(ring_second(pre_act, b0, a0, "y"), -y))
        b3, a3, pre_all = tie((b3, a3, pre_all))
        active, slope = gelu_parts(pre_all.astype(f32))
        act_all = active.astype(bf16)
    half = 4 * kd
    with jax.named_scope("og_x2"):
        slots = tie(ring_second(og, b3, a3, "x"))
        og = jnp.concatenate(turned(slots, -x - y))
    with jax.named_scope("og_y"):
        pieces = [(og[:, r * kd : (r + 1) * kd], og[:, half + r * kd : half + (r + 1) * kd]) for r in range(4)]
        pieces = [jnp.where(first, jnp.concatenate([u, v], 1), jnp.concatenate([v, u], 1)) for u, v in pieces]
        og_h = jnp.concatenate(turned(pieces, -zl), 1)
        b5, a5 = ring_first(og_h, "y")
    with jax.named_scope("down"):
        blocks = product(og[:, :half], og[:, half:], act_all)
        blocks, tok = tie((blocks, tok))
        parts = [shift(blocks[r].astype(bf16), "zl", r) for r in (1, 3)]
    with jax.named_scope("tok_x"):
        b4, a4 = ring_first(tok, "x")
        b5, a5, parts, b4, a4 = tie((b5, a5, parts, b4, a4))

    def term(v, r):
        w_r = lax.dynamic_slice_in_dim(w_all, (y + r) % 4 * 2 * half, 2 * half, 0)
        return jnp.dot(v, w_r, preferred_element_type=f32)

    with jax.named_scope("og_y2"):
        near = b5.shape[0] // 2
        far = [shift(b5[:near], "y", 1), shift(a5[near:], "y", -1)]
    with jax.named_scope("hid"):
        hid = term(og_h, 0)
        hid, b4, a4, blocks[2] = tie((hid, b4, a4, blocks[2]))
    with jax.named_scope("down"):
        parts.append(shift(blocks[2].astype(bf16), "zl", 2))
    with jax.named_scope("tok_x2"):
        toks = ring_second(tok, b4, a4, "x")
    with jax.named_scope("hid"):
        hid = hid + term(a5, 1) + term(b5, 3)
        hid, far, parts[2], toks = tie((hid, far, parts[2], toks))
        hid = hid + term(jnp.concatenate(far), 2)
        pre_grad = (hid * slope).astype(bf16)
    with jax.named_scope("up"):
        tok = jnp.concatenate(turned(toks, -x - y))
        up = product(tok[:, :half], tok[:, half:], pre_grad, bf16)
        down = total_of(blocks[0], parts)
        up = total_of(up[0], spread(up))
    return (up, down)


def solution(mesh):
    fine = Mesh(mesh.devices.reshape(4, 4, 2, 2, 4), ROW + COL)
    return jax.shard_map(
        body,
        mesh=fine,
        in_specs=(P(None, ROW), P(COL, ROW), P(ROW, COL), P(ROW, COL)),
        out_specs=(P(ROW, COL), P(ROW, COL)),
        check_vma=False,
    )
```
